256 devices in a mesh: prow: 32 (over z, x), pcol: 8 (over y, core).
Axes of the slice: x: 4, y: 4, z: 8, core: 2. Of those that a mesh axis runs over, the one named last changes fastest.
Arguments:
- matrix: float32 [16384, 24576], P('prow', 'pcol'), may hold values from -3 to 3
- pivots: int32 [256], replicated, may hold values from 128 to 16383, as said below
- lower_inverse: float32 [2, 128, 128], replicated, may hold values from -0.5 to 0.5
- upper_inverse: float32 [2, 128, 128], replicated, may hold values from -0.09375 to 0.09375
Outputs:
- factored: float32 [16384, 24576], P('prow', 'pcol')
The draws below stay inside these ranges and needn't reach their ends.
Inputs may be any that keep to these rules, and one draw needn't show every extreme that they name: For each section t, the entries pivots[t * 128] to pivots[(t + 1) * 128 - 1] are distinct and lie between (t + 1) * 128 and 16383.
All inputs are finite; a program needn't handle non-finite values.
Results may differ from the reference program's by a relative error of at most 0.0003.
Values sent between devices are 32-bit elements; how exact they have to be, the bound alone decides.
A program may use at most 64 MiB of HBM per device.

```python
import jax
import jax.numpy as jnp
from jax import lax

NB = 128
NC = 24576
R_DEV = 512
C_DEV = 3072
NR = 16384
N_PROW = 32
N_PCOL = 8


def draw_pivots(key, part):
    key = jax.random.fold_in(key, 5)
    slot_ids = jnp.arange(NB, dtype=jnp.int32)
    sections = []
    for section in range(2):
        section_key = jax.random.fold_in(key, section + 1)
        lowest = (section + 1) * NB
        span = NR - lowest - 2
        chosen = jax.random.permutation(jax.random.fold_in(section_key, 1), span)[:NB].astype(jnp.int32) + lowest + 1
        slots = jax.random.permutation(jax.random.fold_in(section_key, 2), NB).astype(jnp.int32)
        chosen = jnp.where(slot_ids == slots[0], NR - 1, chosen)
        chosen = jnp.where(slot_ids == slots[1], lowest, chosen)
        sections.append(chosen.astype(jnp.int32))
    return jnp.concatenate(sections).astype(jnp.int32)


def block_levels(key, extent, cuts, low, largest):
    def one(dim, blocks):
        steps = jax.random.uniform(jax.random.fold_in(jax.random.fold_in(key, 6), dim), (blocks,), jnp.float32, low / len(cuts), largest / len(cuts))
        return jnp.repeat(jnp.exp(steps), extent[dim] // blocks).reshape((-1,) + (1,) * (len(extent) - dim - 1))

    loudness = one(*cuts[0])
    for cut in cuts[1:]:
        loudness = loudness * one(*cut)
    return loudness


def scatter_about(key, dims, deviation, bound, cuts=(), kind=jnp.bfloat16):
    array = jax.random.normal(key, dims, jnp.float32) * deviation
    if len(cuts) > 0:
        array = block_levels(key, dims, cuts, -0.22, 0.18) * array
    return jnp.clip(array, min=-bound, max=bound).astype(kind)


def setup_inputs(seed: int = 0) -> dict:
    key_list = jax.random.split(jax.random.key(seed), 5)
    matrix = scatter_about(key_list[0], (NR, NC), 0.5, 3.0, ((0, 32), (1, 8)), jnp.float32)
    pivots = draw_pivots(jax.random.fold_in(key_list[4], 71), 0)
    lower_inverse = scatter_about(key_list[2], (2, NB, NB), NB ** -0.5, 0.5, (), jnp.float32)
    upper_inverse = scatter_about(key_list[3], (2, NB, NB), (32 * NB) ** -0.5, 0.09375, (), jnp.float32)
    return {"matrix": matrix, "pivots": pivots, "lower_inverse": lower_inverse, "upper_inverse": upper_inverse}


def row_place(glob):
    return ((glob // NB) % N_PROW) * R_DEV + (glob // NB // N_PROW) * NB + glob % NB


def col_place(glob):
    return ((glob // NB) % N_PCOL) * C_DEV + (glob // NB // N_PCOL) * NB + glob % NB


def compose(section, pivots):
    def swap_one(column, source_of):
        first = section * NB + column
        second = pivots[first]
        first_src = source_of[first]
        second_src = source_of[second]
        return source_of.at[first].set(second_src).at[second].set(first_src)
    return lax.fori_loop(0, NB, swap_one, jnp.arange(NR, dtype=jnp.int32))


def reference(matrix, pivots, lower_inverse, upper_inverse):
    stored = jnp.arange(NR, dtype=jnp.int32)
    glob_rows = (((stored % R_DEV) // NB) * N_PROW + stored // R_DEV) * NB + stored % NB
    stored_cols = jnp.arange(NC, dtype=jnp.int32)
    glob_cols = (((stored_cols % C_DEV) // NB) * N_PCOL + stored_cols // C_DEV) * NB + stored_cols % NB
    work = matrix
    block_ids = jnp.arange(NB, dtype=jnp.int32)
    for section in range(2):
        source_of = compose(section, pivots)
        work = work[row_place(source_of[glob_rows]).astype(jnp.int32)]
        top_rows = row_place(section * NB + block_ids).astype(jnp.int32)
        panel_columns = col_place(section * NB + block_ids).astype(jnp.int32)
        lower_unit = jnp.tril(lower_inverse[section], -1) + jnp.eye(NB, dtype=jnp.float32)
        upper_tri = jnp.triu(upper_inverse[section])
        upper_rows = jnp.dot(lower_unit, work[top_rows], precision=lax.Precision.HIGHEST)
        panel = jnp.dot(work[:, panel_columns], upper_tri, precision=lax.Precision.HIGHEST)
        beneath = glob_rows >= (section + 1) * NB
        rightward = glob_cols >= (section + 1) * NB

        def update_slab(pieces):
            slab_rows, slab_panel, slab_beneath = pieces
            updated = slab_rows - jnp.dot(slab_panel, upper_rows, precision=lax.Precision.HIGHEST)
            return jnp.where(slab_beneath[:, None] & rightward[None, :], updated, slab_rows)

        work = lax.map(update_slab, (work.reshape(N_PROW, R_DEV, NC), panel.reshape(N_PROW, R_DEV, NB), beneath.reshape(N_PROW, R_DEV))).reshape(NR, NC)
        work = work.at[:, panel_columns].set(jnp.where(beneath[:, None], panel, work[:, panel_columns]))
        work = work.at[top_rows].set(jnp.where(rightward[None, :], upper_rows, work[top_rows]))
    return work
```

```python
import functools

import jax
import jax.numpy as jnp
from jax import lax
from jax.experimental import pallas as pl
from jax.experimental.pallas import tpu as pltpu
from jax.sharding import PartitionSpec as P

MESH = pl.DeviceIdType.MESH
NB = 128
ROWS = 512
COLS = 3072
NPROW = 32
REACH_R = 3
REACH_T = 5
GROUPS_R = 2 * REACH_R + 1
GROUPS_T = 2 * REACH_T + 1
TROWS = 8 * GROUPS_T
EXT = ROWS + 256 + TROWS
F32 = jnp.float32
BF16 = jnp.bfloat16


def hp(a, b):
    return jnp.dot(a, b, precision=lax.Precision.HIGHEST, preferred_element_type=F32)


def owner_of(row):
    return (row // NB) % NPROW


def local_of(row):
    return row // (NB * NPROW) * NB + row % NB


def wrapped(distance):
    return (distance + 16) % NPROW - 16


def ranks(key):
    return jnp.sum((key[None, :] < key[:, None]).astype(jnp.int32), axis=1)


def plan(pivots, p):
    ids = jnp.arange(NB, dtype=jnp.int32)
    piv0, piv1 = pivots[:NB], pivots[NB:]
    same = piv1[:, None] == piv0[None, :]
    onto = piv0[:, None] - NB == ids[None, :]
    src1 = jnp.where(same.any(1), jnp.sum(jnp.where(same, ids[None, :], 0), 1), piv1)
    src = jnp.concatenate([piv0, src1])
    via = jnp.sum(jnp.where(onto, piv1[None, :], 0), 1)
    dest0 = jnp.where(piv0 < 2 * NB, via, jnp.where(same.any(0), -1, piv0))
    dest1 = jnp.where(onto.any(0), -1, piv1)

    own, local = owner_of(src), local_of(src)
    rank = ranks(own * 256 + jnp.arange(256, dtype=jnp.int32))
    skew = 16 * own + 7 - 2 * rank
    slot = (rank + (jnp.max(skew) + jnp.min(skew)) // 4) % 256
    fits = jnp.all(jnp.abs(wrapped(slot // 8 - own)) <= REACH_R)
    wanted = (8 * (p - REACH_R) + jnp.arange(8 * GROUPS_R, dtype=jnp.int32)) % 256
    mine = (slot[None, :] == wanted[:, None]) & (own == p)[None, :]
    index = jnp.sum(jnp.where(mine, local[None, :] + 1, 0), 1) - 1
    slot_hot = (slot[:, None] == jnp.arange(256)[None, :]).astype(F32)

    row_hots, group_hots, orders = [], [], []
    for section, dest in enumerate((dest0, dest1)):
        moves = dest >= 0
        to = jnp.where(moves, owner_of(dest), ids // 4)
        rank = ranks(to * NB + ids)
        skew = 8 * to + 3 - 2 * rank
        place = (rank + (jnp.max(skew) + jnp.min(skew)) // 4) % NB
        group = place // 8
        home = group // 2 * 4 + jnp.where(group % 2 == 0, section, 3 - section)
        fits = fits & jnp.all((jnp.abs(wrapped(to - home)) <= REACH_T) | ~moves)
        column = (home - p + REACH_T) % NPROW * 8 + place % 8
        here = moves & (to == p)
        row_hots.append(hot((local_of(dest)[None, :] == jnp.arange(ROWS)[:, None]) & here[None, :]))
        group_hots.append(hot(column[:, None] == jnp.arange(TROWS)[None, :]))
        orders.append((place[None, :] == ids[:, None]).astype(F32))
    put = jnp.dot(jnp.concatenate(row_hots, 1), jnp.concatenate(group_hots, 0), preferred_element_type=F32)
    order = jnp.where(p == 0, orders[0], orders[1])
    return fits, index, order, slot_hot, put


def hot(mask):
    return mask.astype(BF16)


A_CHUNKS = ((0, 128, 1), (128, 512, -1), (640, 640, 1))
B_CHUNKS = ((1280, 896, 1), (2176, 896, -1))
SHIFTS = ((0, 128), (1280, 1792), (128, 1152))
T_CHUNKS = ((0, 128), (128, 2944))
COPIES = 224


def hops(long, way):
    return 4 if long == way else 3


def gather_kernel(index_ref, order_ref, a_hbm, r_ref, t_ref, e_ref, a_ref, pack, inbox, t_pack, load_sem, send_sem, recv_sem):
    p, q = lax.axis_index("prow"), lax.axis_index("pcol")
    z, x = lax.div(p, 4), lax.rem(p, 4)
    y, core = lax.div(q, 2), lax.rem(q, 2)
    source = p < 2
    sends, receipts = {}, {}
    pending = []

    def number(numbers, tag):
        assert len(numbers) < COPIES or tag in numbers
        return numbers.setdefault(tag, len(numbers))

    def copy(src, dst, tag, device, recv_tag=None):
        return pltpu.make_async_remote_copy(
            src_ref=src,
            dst_ref=dst,
            send_sem=send_sem.at[number(sends, tag)],
            recv_sem=recv_sem.at[number(receipts, recv_tag or tag)],
            device_id=device,
            device_id_type=MESH,
        )

    def send(src, dst, tag, device):
        c = copy(src, dst, tag, device)
        c.start()
        pending.append(c)

    def arrived(dst, tag):
        copy(dst, dst, tag, core_peer).wait_recv()

    def along(step):
        return lax.rem(p + step + NPROW, NPROW), q

    def at_z(step):
        return lax.rem(z + step + 8, 8) * 4 + x, q

    def at_x(step):
        return z * 4 + lax.rem(x + step + 4, 4), q

    core_peer = (p, y * 2 + 1 - core)

    def block(zz, xx, cols):
        start = pl.multiple_of((lax.rem(z + zz + 8, 8) * 4 + lax.rem(x + xx + 4, 4)) * 8, 8)
        return r_ref.at[pl.ds(start, 8), pl.ds(cols[0], cols[1])]

    def plane(zz, cols):
        start = pl.multiple_of(lax.rem(z + zz + 8, 8) * 32, 32)
        return r_ref.at[pl.ds(start, 32), pl.ds(cols[0], cols[1])]

    load = pltpu.make_async_copy(a_hbm, a_ref, load_sem.at[0])
    load.start()

    barrier = pltpu.get_barrier_semaphore()

    def greet(device):
        pl.semaphore_signal(barrier, inc=1, device_id=device, device_id_type=MESH)

    for step in range(-REACH_T, REACH_T + 1):
        if step:
            greet(along(step))
    greet(core_peer)

    @pl.when(y > 0)
    def _():
        greet((p, core))

    from_row = jnp.where((x == 0) | (x == 3), 0, 1)

    @pl.when(p != from_row)
    def _():
        greet((from_row, q))

    load.wait()

    def take(m, carry):
        r = index_ref[m]
        row = a_ref[pl.ds(jnp.maximum(r, 0), 1), :]
        pack[pl.ds(m, 1), :] = jnp.where(r >= 0, row, 0.0)
        return carry

    lax.fori_loop(0, 8 * GROUPS_R, take, 0)
    pl.semaphore_wait(barrier, 2 * REACH_T + 1 + jnp.where(y == 0, 3, 0) + jnp.where(source, 15, 0))

    def shift(cols):
        at = pl.ds(*cols)
        for d in range(-REACH_R, REACH_R + 1):
            if d:
                send(pack.at[pl.ds(8 * (d + REACH_R), 8), at], inbox.at[pl.ds(8 * (REACH_R - d), 8), at], ("shift", cols, d), along(d))

    def settle(cols):
        at = pl.ds(*cols)
        for d in range(-REACH_R, REACH_R + 1):
            if d:
                arrived(inbox.at[pl.ds(8 * (REACH_R - d), 8), at], ("shift", cols, d))
        total = pack[8 * REACH_R : 8 * REACH_R + 8, at]
        for d in range(-REACH_R, REACH_R + 1):
            if d:
                total = total + inbox[8 * (REACH_R - d) : 8 * (REACH_R - d) + 8, at]
        r_ref[pl.ds(pl.multiple_of(p * 8, 8), 8), at] = total

    ext_a = e_ref.at[core, pl.ds(0, ROWS)]
    ext_rt = e_ref.at[core, pl.ds(ROWS, EXT - ROWS)]
    far_a = e_ref.at[1 - core, pl.ds(0, ROWS)]
    far_rt = e_ref.at[1 - core, pl.ds(ROWS, EXT - ROWS)]

    shift(SHIFTS[0])

    @pl.when(y == 0)
    def _():
        e_ref[core, :ROWS] = a_ref[:, :NB]
        for step in (1, 3, 2):
            copy(ext_a, ext_a, ("ya", step), (p, step * 2 + core), ("ya",)).start()

    shift(SHIFTS[1])
    shift(SHIFTS[2])

    own_t = pl.ds(8 * REACH_T, 8)

    @pl.when(source)
    def _():
        def turn(n, carry):
            at = pl.ds(pl.multiple_of(n * 512, 512), 512)
            t_pack[:, at] = hp(order_ref[...], a_ref[:NB, at])
            return carry

        lax.fori_loop(0, COLS // 512, turn, 0)
        for cols in T_CHUNKS:
            at = pl.ds(*cols)
            for g in range(1, 16):
                to = g // 2 * 4 + (p if g % 2 == 0 else 3 - p)
                copy(t_pack.at[pl.ds(8 * g, 8), at], t_ref.at[own_t, at], ("ts", cols, g), (to, q), ("ts", cols)).start()
        t_ref[own_t, :] = t_pack[:8]

    def spread_x(cols):
        for dx in (1, 3, 2):
            send(block(0, 0, cols), block(0, 0, cols), ("a1", cols, dx), at_x(dx))

    def joined_x(cols):
        for dx in (1, 3, 2):
            arrived(block(0, -dx, cols), ("a1", cols, dx))

    def pass_plane(cols, s):
        for way in (1, -1):
            if s > 0:
                if s > hops(cols[2], way):
                    continue
                arrived(plane(-way * s, cols), ("a2", cols, way, s))
            if s < hops(cols[2], way):
                part = plane(-way * s, cols)
                send(part, part, ("a2", cols, way, s + 1), at_z(way))

    def ways_at(cols, s):
        return [0] if s == 0 else [-way * s for way in (1, -1) if s <= hops(cols[2], way)]

    def pass_block(cols, s):
        for way in (1, -1):
            if s > 0:
                if s > hops(cols[2], way):
                    continue
                arrived(block(-way * s, 0, cols), ("b1", cols, way, s))
            part = block(-way * s, 0, cols)
            if s < hops(cols[2], way):
                send(part, part, ("b1", cols, way, s + 1), at_z(way))
            if s > 0 or way == 1:
                for dx in (1, -1):
                    send(part, part, ("b2", cols, -way * s if s else 0, dx), at_x(dx))

    def relay_x(cols, s):
        for zz in ways_at(cols, s):
            for dx in (1, -1):
                arrived(block(zz, -dx, cols), ("b2", cols, zz, dx))
                if dx == cols[2]:
                    part = block(zz, -dx, cols)
                    send(part, part, ("b3", cols, zz), at_x(dx))

    def end_x(cols, s):
        for zz in ways_at(cols, s):
            arrived(block(zz, 2, cols), ("b3", cols, zz))

    def t_ready(cols):
        at = pl.ds(*cols)

        @pl.when(jnp.logical_not(source))
        def _():
            arrived(t_ref.at[own_t, at], ("ts", cols))

        for e in range(-REACH_T, REACH_T + 1):
            if e:
                send(t_ref.at[own_t, at], t_ref.at[pl.ds(8 * (REACH_T - e), 8), at], ("th", cols, e), along(e))

    def t_done(cols):
        at = pl.ds(*cols)
        for e in range(-REACH_T, REACH_T + 1):
            if e:
                arrived(t_ref.at[pl.ds(8 * (REACH_T - e), 8), at], ("th", cols, e))

    first, *rest = A_CHUNKS
    settle(SHIFTS[0])
    spread_x(first)
    settle(SHIFTS[1])
    for cols in B_CHUNKS:
        pass_block(cols, 0)
    settle(SHIFTS[2])
    for cols in rest:
        spread_x(cols)
    joined_x(first)
    pass_plane(first, 0)
    t_ready(T_CHUNKS[0])
    for cols in rest:
        joined_x(cols)
        pass_plane(cols, 0)
    for s in range(1, 5):
        pass_plane(first, s)
        for cols in B_CHUNKS:
            pass_block(cols, s)
        for cols in rest:
            pass_plane(cols, s)
        for cols in B_CHUNKS:
            relay_x(cols, s - 1)
        if s == 2:
            t_ready(T_CHUNKS[1])
    t_done(T_CHUNKS[0])

    @pl.when(y == 0)
    def _():
        e_ref[core, ROWS : ROWS + 256] = r_ref[:, :NB]
        e_ref[core, ROWS + 256 :] = t_ref[:, :NB]
        for step in (1, 3, 2):
            copy(ext_rt, ext_rt, ("yr", step), (p, step * 2 + core), ("yr",)).start()

    @pl.when(y > 0)
    def _():
        arrived(ext_a, ("ya",))

    send(ext_a, ext_a, ("ca",), core_peer)
    for cols in B_CHUNKS:
        relay_x(cols, 4)

    @pl.when(y > 0)
    def _():
        arrived(ext_rt, ("yr",))

    send(ext_rt, ext_rt, ("cr",), core_peer)
    for s in range(5):
        for cols in B_CHUNKS:
            end_x(cols, s)
    t_done(T_CHUNKS[1])
    arrived(far_a, ("ca",))
    arrived(far_rt, ("cr",))
    for c in pending:
        c.wait_send()

    @pl.when(y == 0)
    def _():
        for step in (1, 3, 2):
            copy(ext_a, ext_a, ("ya", step), (p, step * 2 + core), ("ya",)).wait_send()
            copy(ext_rt, ext_rt, ("yr", step), (p, step * 2 + core), ("yr",)).wait_send()

    @pl.when(source)
    def _():
        for cols in T_CHUNKS:
            at = pl.ds(*cols)
            for g in range(1, 16):
                to = g // 2 * 4 + (p if g % 2 == 0 else 3 - p)
                copy(t_pack.at[pl.ds(8 * g, 8), at], t_ref.at[own_t, at], ("ts", cols, g), (to, q), ("ts", cols)).wait_send()


def gather(matrix, index, order):
    vmem = pl.BlockSpec(memory_space=pltpu.VMEM)
    return pl.pallas_call(
        gather_kernel,
        out_shape=[
            jax.ShapeDtypeStruct((256, COLS), F32),
            jax.ShapeDtypeStruct((TROWS, COLS), F32),
            jax.ShapeDtypeStruct((2, EXT, NB), F32),
        ],
        in_specs=[pl.BlockSpec(memory_space=pltpu.SMEM), vmem, pl.BlockSpec(memory_space=pl.ANY)],
        out_specs=[vmem, vmem, vmem],
        scratch_shapes=[
            pltpu.VMEM((ROWS, COLS), F32),
            pltpu.VMEM((8 * GROUPS_R, COLS), F32),
            pltpu.VMEM((8 * GROUPS_R, COLS), F32),
            pltpu.VMEM((NB, COLS), F32),
            pltpu.SemaphoreType.DMA((1,)),
            pltpu.SemaphoreType.DMA((COPIES,)),
            pltpu.SemaphoreType.DMA((COPIES,)),
        ],
        compiler_params=pltpu.CompilerParams(collective_id=0, has_side_effects=True, vmem_limit_bytes=48 << 20),
        name="gather_rows",
    )(index, order, matrix)


WIDTH = 512


def split(x):
    high = x.astype(BF16)
    return high, (x - high.astype(F32)).astype(BF16)


def finish_kernel(a_ref, r_ref, t_ref, e_ref, put_ref, slot_ref, low_ref, up_ref, o_ref, w_ref, put16_ref, keep_ref, first_ref):
    step = pl.program_id(0)
    p, q = lax.axis_index("prow"), lax.axis_index("pcol")

    @pl.when(step == 0)
    def _():
        row = lax.broadcasted_iota(jnp.int32, (NB, NB), 0)
        col = lax.broadcasted_iota(jnp.int32, (NB, NB), 1)
        lower = [jnp.where(row > col, low_ref[t], jnp.where(row == col, 1.0, 0.0)) for t in range(2)]
        upper = [jnp.where(row <= col, up_ref[t], 0.0) for t in range(2)]
        put = put_ref[...]
        top = lax.broadcasted_iota(jnp.int32, (ROWS, 1), 0) < NB
        at0, at1 = top & (p == 0), top & (p == 1)
        keep = jnp.where(at0 | at1, 0.0, 1.0 - jnp.sum(put, axis=1, keepdims=True))
        keep_ref[...] = jnp.broadcast_to(keep, (ROWS, NB))
        put16_ref[...] = put.astype(BF16)
        pi0, pi1 = slot_ref[:NB], slot_ref[NB:]
        g0, g1 = hp(lower[0], pi0), hp(lower[1], pi1)
        r0, r1 = e_ref[0, ROWS : ROWS + 256], e_ref[1, ROWS : ROWS + 256]
        k0 = hp(r0, upper[0])
        m1 = g1 - hp(hp(g1, k0), g0)
        u01 = hp(g0, r1)
        c0 = keep * e_ref[0, :ROWS] + hp(put, e_ref[0, ROWS + 256 :])
        c1 = keep * e_ref[1, :ROWS] + hp(put, e_ref[1, ROWS + 256 :])
        pis = jnp.where(p == 0, pi0, pi1)
        blank = jnp.zeros((ROWS - NB, NB), F32)
        c0 = jnp.where(at0 | at1, jnp.concatenate([hp(pis, r0), blank], 0), c0)
        c1 = jnp.where(at1, jnp.concatenate([hp(pi1, r1), blank], 0), c1)
        panel0 = hp(c0, upper[0])
        middle = c1 - hp(panel0, u01)
        panel1 = hp(middle, upper[1])
        w = hp(panel0, g0) + hp(panel1, m1)
        blank2 = jnp.zeros((ROWS - NB, 256), F32)
        w = jnp.where(at0 | at1, jnp.concatenate([-jnp.where(p == 0, g0, m1), blank2], 0), w)
        high, low = split(-w)
        w_ref[:, :256] = high
        w_ref[:, 256:512] = high
        w_ref[:, 512:] = low
        u01_tall = jnp.concatenate([u01, blank], 0)
        first0 = jnp.where(at0, c0, panel0)
        first1 = jnp.where(at0, u01_tall, jnp.where(at1, middle, panel1))
        first_ref[...] = jnp.where(q == 0, first0, first1)

    r_high, r_low = split(r_ref[...])
    t_high, t_low = split(t_ref[...])
    dot = functools.partial(jnp.dot, preferred_element_type=F32)
    rows = jnp.concatenate([r_high, r_low, r_high], 0)
    put16 = put16_ref[...]
    moved = dot(put16, t_high) + dot(put16, t_low)
    o_ref[...] = keep_ref[:, :1] * a_ref[...] + (moved + dot(w_ref[...], rows))

    @pl.when((step == 0) & (q < 2))
    def _():
        o_ref[:, :NB] = first_ref[...]


def finish(matrix, rows, tops, ext, put, slot_hot, lower_inverse, upper_inverse):
    whole = lambda *dims: pl.BlockSpec(dims, lambda i: (0,) * len(dims))
    wide = lambda n: pl.BlockSpec((n, WIDTH), lambda i: (0, i))
    return pl.pallas_call(
        finish_kernel,
        grid=(COLS // WIDTH,),
        out_shape=jax.ShapeDtypeStruct((ROWS, COLS), F32),
        in_specs=[wide(ROWS), wide(256), wide(TROWS), whole(2, EXT, NB), whole(ROWS, TROWS), whole(256, 256), whole(2, NB, NB), whole(2, NB, NB)],
        out_specs=wide(ROWS),
        scratch_shapes=[
            pltpu.VMEM((ROWS, 768), BF16),
            pltpu.VMEM((ROWS, TROWS), BF16),
            pltpu.VMEM((ROWS, NB), F32),
            pltpu.VMEM((ROWS, NB), F32),
        ],
        compiler_params=pltpu.CompilerParams(vmem_limit_bytes=48 << 20),
        name="finish",
    )(matrix, rows, tops, ext, put, slot_hot, lower_inverse, upper_inverse)


def broadcast(block, axis, holder):
    block = jnp.where(lax.axis_index(axis) == holder, block, jnp.zeros_like(block))
    return lax.psum(block, axis)


def any_pivots(matrix, pivots, lower_inverse, upper_inverse):
    process_row = lax.axis_index("prow")
    process_col = lax.axis_index("pcol")
    prow_count = lax.axis_size("prow")
    pcol_count = lax.axis_size("pcol")
    rows_dev, cols_dev = matrix.shape
    block = lower_inverse.shape[1]
    row_offsets = jnp.arange(rows_dev, dtype=jnp.int32)
    glob_rows = (row_offsets // block * prow_count + process_row) * block + row_offsets % block
    col_offsets = jnp.arange(cols_dev, dtype=jnp.int32)
    glob_cols = (col_offsets // block * pcol_count + process_col) * block + col_offsets % block
    block_ids = jnp.arange(block, dtype=jnp.int32)
    current = matrix
    for section in range(2):
        wanted = jnp.concatenate(
            [section * block + block_ids, pivots[section * block : (section + 1) * block]]
        )
        owner_row = wanted // block % prow_count
        local_row = wanted // block // prow_count * block + wanted % block
        owned = owner_row == process_row
        picked = jnp.where(owned[:, None], current[local_row], 0.0)
        in_play = lax.psum(picked, "prow")
        arrived = jnp.concatenate([in_play[block:], in_play[:block]], axis=0)
        current = current.at[jnp.where(owned, local_row, rows_dev)].set(arrived, mode="drop")
        lower_unit = jnp.tril(lower_inverse[section], -1) + jnp.eye(block, dtype=jnp.float32)
        upper_tri = jnp.triu(upper_inverse[section])
        upper_rows = jnp.dot(lower_unit, arrived[:block], precision=lax.Precision.HIGHEST)
        panel_block = current[:, :block]
        solved = jnp.dot(panel_block, upper_tri, precision=lax.Precision.HIGHEST)
        panel = broadcast(solved, "pcol", section)
        beneath = glob_rows >= (section + 1) * block
        rightward = glob_cols >= (section + 1) * block
        updated = current - jnp.dot(panel, upper_rows, precision=lax.Precision.HIGHEST)
        current = jnp.where(beneath[:, None] & rightward[None, :], updated, current)
        panel_owner = process_col == section
        current = current.at[:, :block].set(
            jnp.where(beneath[:, None] & panel_owner, panel, current[:, :block])
        )
        block_owner = process_row == section
        current = current.at[:block].set(
            jnp.where(block_owner & rightward[None, :], upper_rows, current[:block])
        )
    return current


def spread(matrix, lower_inverse, upper_inverse, index, order, slot_hot, put):
    rows, tops, ext = gather(matrix, index, order)
    return finish(matrix, rows, tops, ext, put, slot_hot, lower_inverse, upper_inverse)


def shards(matrix, pivots, lower_inverse, upper_inverse):
    p = lax.axis_index("prow")
    fits, index, order, slot_hot, put = plan(pivots, p)
    return lax.cond(
        fits,
        lambda: spread(matrix, lower_inverse, upper_inverse, index, order, slot_hot, put),
        lambda: any_pivots(matrix, pivots, lower_inverse, upper_inverse),
    )


def solution(mesh):
    placed = (P("prow", "pcol"), P(), P(), P())
    return jax.shard_map(
        shards, mesh=mesh, in_specs=placed, out_specs=P("prow", "pcol"), check_vma=False
    )
```

```python
import functools

import jax
import jax.numpy as jnp
from jax import lax
from jax.experimental import pallas as pl
from jax.experimental.pallas import tpu as pltpu
from jax.sharding import PartitionSpec as P

MESH = pl.DeviceIdType.MESH
NB = 128
ROWS = 512
COLS = 3072
NPROW = 32
REACH_R = 3
REACH_T = 5
GROUPS_R = 2 * REACH_R + 1
GROUPS_T = 2 * REACH_T + 1
TROWS = 8 * GROUPS_T
EXT = ROWS + 256 + TROWS
F32 = jnp.float32
BF16 = jnp.bfloat16
I32 = jnp.int32


def hp(a, b):
    return jnp.dot(a, b, precision=lax.Precision.HIGHEST, preferred_element_type=F32)


def hot(mask):
    return jnp.where(mask, 1.0, 0.0).astype(F32)


def owner_of(row):
    return (row >> 7) & (NPROW - 1)


def local_of(row):
    return ((row >> 12) << 7) + (row & (NB - 1))


def wrapped(distance):
    return ((distance + 16) & (NPROW - 1)) - 16


def iota(shape, dim):
    return lax.broadcasted_iota(I32, shape, dim)


def both(row):
    n = row.shape[1]
    eye = iota((n, n), 0) == iota((n, n), 1)
    return row, jnp.sum(jnp.where(eye, row, 0), axis=1, keepdims=True)


def ranked(row, col):
    n = row.shape[1]
    key_row, key_col = row * n + iota((1, n), 1), col * n + iota((n, 1), 0)
    in_row = jnp.sum(jnp.where(key_col < key_row, 1, 0), axis=0, keepdims=True)
    in_col = jnp.sum(jnp.where(key_row < key_col, 1, 0), axis=1, keepdims=True)
    return in_row, in_col


def plan_kernel(piv_ref, fits_ref, meta_ref, index_ref, order_ref, slot_ref, put_ref):
    p = lax.axis_index("prow")
    r0, r1 = piv_ref[0:1, :], piv_ref[1:2, :]
    c0 = both(r0)[1]
    line, lane = iota((NB, NB), 0), iota((NB, NB), 1)
    same = c0 == r1
    onto = c0 - NB == lane
    same_i, onto_i = jnp.where(same, 1, 0), jnp.where(onto, 1, 0)
    src1 = jnp.where(jnp.max(same_i, axis=0, keepdims=True) > 0, jnp.sum(same_i * line, axis=0, keepdims=True), r1)
    via = jnp.sum(jnp.where(onto, r1, 0), axis=1, keepdims=True)
    dest0_col = jnp.where(c0 < 2 * NB, via, jnp.where(jnp.max(same_i, axis=1, keepdims=True) > 0, -1, c0))
    dest0 = jnp.sum(jnp.where(line == lane, dest0_col, 0), axis=0, keepdims=True)
    dest1, dest1_col = both(jnp.where(jnp.max(onto_i, axis=0, keepdims=True) > 0, -1, r1))
    meta_ref[0:1, :] = r0
    meta_ref[1:2, :] = src1
    meta_ref[2:3, :] = dest0
    meta_ref[3:4, :] = dest1
    meta_ref[4:8, :] = jnp.zeros((4, NB), I32)

    src, src_col = jnp.concatenate([r0, src1], 1), jnp.concatenate([c0, both(src1)[1]], 0)
    own, own_col = owner_of(src), owner_of(src_col)
    rank, rank_col = ranked(own, own_col)
    skew = 16 * own + 7 - 2 * rank
    turn = (jnp.max(skew, axis=1, keepdims=True) + jnp.min(skew, axis=1, keepdims=True)) >> 2
    slot, slot_col = (rank + turn) & 255, (rank_col + turn) & 255
    off_r = jnp.max(jnp.abs(wrapped((slot >> 3) - own)))
    wanted = (8 * (p - REACH_R) + iota((1, NB), 1)) & 255
    mine = (slot_col == wanted) & (own_col == p)
    index_ref[0:1, :] = jnp.sum(jnp.where(mine, local_of(src_col) + 1, 0), axis=0, keepdims=True) - 1
    slot_ref[...] = hot(slot_col == iota((256, 256), 1))

    put = jnp.zeros((ROWS, NB), F32)
    off_t = 0
    for section, (dest, dest_col) in enumerate(((dest0, dest0_col), (dest1, dest1_col))):
        to = jnp.where(dest >= 0, owner_of(dest), iota((1, NB), 1) >> 2)
        to_col = jnp.where(dest_col >= 0, owner_of(dest_col), iota((NB, 1), 0) >> 2)
        rank, rank_col = ranked(to, to_col)
        skew = 8 * to + 3 - 2 * rank
        turn = (jnp.max(skew, axis=1, keepdims=True) + jnp.min(skew, axis=1, keepdims=True)) >> 2
        place, place_col = (rank + turn) & (NB - 1), (rank_col + turn) & (NB - 1)
        home, home_col = (
            (v >> 4) * 4 + jnp.where(((v >> 3) & 1) == 0, section, 3 - section) for v in (place, place_col)
        )
        off_t = jnp.maximum(off_t, jnp.max(jnp.where(dest >= 0, jnp.abs(wrapped(to - home)), 0)))
        column = ((home_col - p + REACH_T) & (NPROW - 1)) * 8 + (place_col & 7)
        here = (dest >= 0) & (to == p)
        into = hot((local_of(dest) == iota((ROWS, NB), 0)) & here)
        put = put + jnp.dot(into, hot(column == lane), preferred_element_type=F32)

        @pl.when((p == section) | (section == 1) & (p > 1))
        def _():
            order_ref[...] = hot(place == line)

    put_ref[...] = put[:, :TROWS]
    fits_ref[0] = jnp.where((off_r <= REACH_R) & (off_t <= REACH_T), 1, 0)


def plan(pivots):
    vmem = pl.BlockSpec(memory_space=pltpu.VMEM)
    return pl.pallas_call(
        plan_kernel,
        out_shape=[
            jax.ShapeDtypeStruct((1,), I32),
            jax.ShapeDtypeStruct((8, NB), I32),
            jax.ShapeDtypeStruct((1, NB), I32),
            jax.ShapeDtypeStruct((NB, NB), F32),
            jax.ShapeDtypeStruct((256, 256), F32),
            jax.ShapeDtypeStruct((ROWS, TROWS), F32),
        ],
        in_specs=[vmem],
        out_specs=[pl.BlockSpec(memory_space=pltpu.SMEM), vmem, vmem, vmem, vmem, vmem],
        name="plan",
    )(pivots.reshape(2, NB))


A_CHUNKS = ((0, 128, 1), (128, 512, -1), (640, 640, 1))
B_CHUNKS = ((1280, 896, 1), (2176, 896, -1))
SHIFTS = ((0, 128), (1280, 1792), (128, 1152))
T_CHUNKS = ((0, 128), (128, 2944))
COPIES = 224


def hops(long, way):
    return 4 if long == way else 3


def gather_kernel(
    index_ref, order_ref, slot_ref, put_ref, low_ref, up_ref, a_hbm,
    r_ref, t_ref, w_ref, put16_ref, keep_ref, first_ref,
    a_ref, pack, inbox, t_pack, e_ref, load_sem, send_sem, recv_sem,
):
    p, q = lax.axis_index("prow"), lax.axis_index("pcol")
    z, x = lax.div(p, 4), lax.rem(p, 4)
    y, core = lax.div(q, 2), lax.rem(q, 2)
    source = p < 2
    sends, receipts = {}, {}
    pending = []

    def number(numbers, tag):
        assert len(numbers) < COPIES or tag in numbers
        return numbers.setdefault(tag, len(numbers))

    def copy(src, dst, tag, device, recv_tag=None):
        return pltpu.make_async_remote_copy(
            src_ref=src,
            dst_ref=dst,
            send_sem=send_sem.at[number(sends, tag)],
            recv_sem=recv_sem.at[number(receipts, recv_tag or tag)],
            device_id=device,
            device_id_type=MESH,
        )

    def send(src, dst, tag, device):
        c = copy(src, dst, tag, device)
        c.start()
        pending.append(c)

    def arrived(dst, tag):
        copy(dst, dst, tag, core_peer).wait_recv()

    def along(step):
        return lax.rem(p + step + NPROW, NPROW), q

    def at_z(step):
        return lax.rem(z + step + 8, 8) * 4 + x, q

    def at_x(step):
        return z * 4 + lax.rem(x + step + 4, 4), q

    core_peer = (p, y * 2 + 1 - core)

    def block(zz, xx, cols):
        start = pl.multiple_of((lax.rem(z + zz + 8, 8) * 4 + lax.rem(x + xx + 4, 4)) * 8, 8)
        return r_ref.at[pl.ds(start, 8), pl.ds(cols[0], cols[1])]

    def plane(zz, cols):
        start = pl.multiple_of(lax.rem(z + zz + 8, 8) * 32, 32)
        return r_ref.at[pl.ds(start, 32), pl.ds(cols[0], cols[1])]

    load = pltpu.make_async_copy(a_hbm, a_ref, load_sem.at[0])
    load.start()

    barrier = pltpu.get_barrier_semaphore()

    def greet(device):
        pl.semaphore_signal(barrier, inc=1, device_id=device, device_id_type=MESH)

    for step in range(-REACH_T, REACH_T + 1):
        if step:
            greet(along(step))
    greet(core_peer)

    @pl.when(y > 0)
    def _():
        greet((p, core))

    from_row = jnp.where((x == 0) | (x == 3), 0, 1)

    @pl.when(p != from_row)
    def _():
        greet((from_row, q))

    load.wait()

    def take(m, carry):
        r = index_ref[0, m]
        row = a_ref[pl.ds(jnp.maximum(r, 0), 1), :]
        pack[pl.ds(m, 1), :] = jnp.where(r >= 0, row, 0.0)
        return carry

    lax.fori_loop(0, 8 * GROUPS_R, take, 0)
    pl.semaphore_wait(barrier, 2 * REACH_T + 1 + jnp.where(y == 0, 3, 0) + jnp.where(source, 15, 0))

    def shift(cols):
        at = pl.ds(*cols)
        for d in range(-REACH_R, REACH_R + 1):
            if d:
                send(pack.at[pl.ds(8 * (d + REACH_R), 8), at], inbox.at[pl.ds(8 * (REACH_R - d), 8), at], ("shift", cols, d), along(d))

    def settle(cols):
        at = pl.ds(*cols)
        for d in range(-REACH_R, REACH_R + 1):
            if d:
                arrived(inbox.at[pl.ds(8 * (REACH_R - d), 8), at], ("shift", cols, d))
        total = pack[8 * REACH_R : 8 * REACH_R + 8, at]
        for d in range(-REACH_R, REACH_R + 1):
            if d:
                total = total + inbox[8 * (REACH_R - d) : 8 * (REACH_R - d) + 8, at]
        r_ref[pl.ds(pl.multiple_of(p * 8, 8), 8), at] = total

    ext_a = e_ref.at[core, pl.ds(0, ROWS)]
    ext_rt = e_ref.at[core, pl.ds(ROWS, EXT - ROWS)]
    far_a = e_ref.at[1 - core, pl.ds(0, ROWS)]
    far_rt = e_ref.at[1 - core, pl.ds(ROWS, EXT - ROWS)]

    shift(SHIFTS[0])

    @pl.when(y == 0)
    def _():
        e_ref[core, :ROWS] = a_ref[:, :NB]
        for step in (1, 3, 2):
            copy(ext_a, ext_a, ("ya", step), (p, step * 2 + core), ("ya",)).start()

    shift(SHIFTS[1])
    shift(SHIFTS[2])

    own_t = pl.ds(8 * REACH_T, 8)

    @pl.when(source)
    def _():
        def turn(n, carry):
            at = pl.ds(pl.multiple_of(n * 512, 512), 512)
            t_pack[:, at] = hp(order_ref[...], a_ref[:NB, at])
            return carry

        lax.fori_loop(0, COLS // 512, turn, 0)
        for cols in T_CHUNKS:
            at = pl.ds(*cols)
            for g in range(1, 16):
                to = g // 2 * 4 + (p if g % 2 == 0 else 3 - p)
                copy(t_pack.at[pl.ds(8 * g, 8), at], t_ref.at[own_t, at], ("ts", cols, g), (to, q), ("ts", cols)).start()
        t_ref[own_t, :] = t_pack[:8]

    def spread_x(cols):
        for dx in (1, 3, 2):
            send(block(0, 0, cols), block(0, 0, cols), ("a1", cols, dx), at_x(dx))

    def joined_x(cols):
        for dx in (1, 3, 2):
            arrived(block(0, -dx, cols), ("a1", cols, dx))

    def pass_plane(cols, s):
        for way in (1, -1):
            if s > 0:
                if s > hops(cols[2], way):
                    continue
                arrived(plane(-way * s, cols), ("a2", cols, way, s))
            if s < hops(cols[2], way):
                part = plane(-way * s, cols)
                send(part, part, ("a2", cols, way, s + 1), at_z(way))

    def ways_at(cols, s):
        return [0] if s == 0 else [-way * s for way in (1, -1) if s <= hops(cols[2], way)]

    def pass_block(cols, s):
        for way in (1, -1):
            if s > 0:
                if s > hops(cols[2], way):
                    continue
                arrived(block(-way * s, 0, cols), ("b1", cols, way, s))
            part = block(-way * s, 0, cols)
            if s < hops(cols[2], way):
                send(part, part, ("b1", cols, way, s + 1), at_z(way))
            if s > 0 or way == 1:
                for dx in (1, -1):
                    send(part, part, ("b2", cols, -way * s if s else 0, dx), at_x(dx))

    def relay_x(cols, s):
        for zz in ways_at(cols, s):
            for dx in (1, -1):
                arrived(block(zz, -dx, cols), ("b2", cols, zz, dx))
                if dx == cols[2]:
                    part = block(zz, -dx, cols)
                    send(part, part, ("b3", cols, zz), at_x(dx))

    def end_x(cols, s):
        for zz in ways_at(cols, s):
            arrived(block(zz, 2, cols), ("b3", cols, zz))

    def t_ready(cols):
        at = pl.ds(*cols)

        @pl.when(jnp.logical_not(source))
        def _():
            arrived(t_ref.at[own_t, at], ("ts", cols))

        for e in range(-REACH_T, REACH_T + 1):
            if e:
                send(t_ref.at[own_t, at], t_ref.at[pl.ds(8 * (REACH_T - e), 8), at], ("th", cols, e), along(e))

    def t_done(cols):
        at = pl.ds(*cols)
        for e in range(-REACH_T, REACH_T + 1):
            if e:
                arrived(t_ref.at[pl.ds(8 * (REACH_T - e), 8), at], ("th", cols, e))

    first, *rest = A_CHUNKS
    settle(SHIFTS[0])
    spread_x(first)
    settle(SHIFTS[1])
    for cols in B_CHUNKS:
        pass_block(cols, 0)
    settle(SHIFTS[2])
    for cols in rest:
        spread_x(cols)
    joined_x(first)
    pass_plane(first, 0)
    t_ready(T_CHUNKS[0])
    for cols in rest:
        joined_x(cols)
        pass_plane(cols, 0)
    for s in range(1, 5):
        pass_plane(first, s)
        for cols in B_CHUNKS:
            pass_block(cols, s)
        for cols in rest:
            pass_plane(cols, s)
        for cols in B_CHUNKS:
            relay_x(cols, s - 1)
        if s == 2:
            t_ready(T_CHUNKS[1])
    t_done(T_CHUNKS[0])

    @pl.when(y == 0)
    def _():
        e_ref[core, ROWS : ROWS + 256] = r_ref[:, :NB]
        e_ref[core, ROWS + 256 :] = t_ref[:, :NB]
        for step in (1, 3, 2):
            copy(ext_rt, ext_rt, ("yr", step), (p, step * 2 + core), ("yr",)).start()

    @pl.when(y > 0)
    def _():
        arrived(ext_a, ("ya",))

    send(ext_a, ext_a, ("ca",), core_peer)
    for cols in B_CHUNKS:
        relay_x(cols, 4)

    @pl.when(y > 0)
    def _():
        arrived(ext_rt, ("yr",))

    send(ext_rt, ext_rt, ("cr",), core_peer)
    arrived(far_a, ("ca",))
    arrived(far_rt, ("cr",))
    weigh(e_ref, put_ref, slot_ref, low_ref, up_ref, w_ref, put16_ref, keep_ref, first_ref)
    for s in range(5):
        for cols in B_CHUNKS:
            end_x(cols, s)
    t_done(T_CHUNKS[1])
    for c in pending:
        c.wait_send()

    @pl.when(y == 0)
    def _():
        for step in (1, 3, 2):
            copy(ext_a, ext_a, ("ya", step), (p, step * 2 + core), ("ya",)).wait_send()
            copy(ext_rt, ext_rt, ("yr", step), (p, step * 2 + core), ("yr",)).wait_send()

    @pl.when(source)
    def _():
        for cols in T_CHUNKS:
            at = pl.ds(*cols)
            for g in range(1, 16):
                to = g // 2 * 4 + (p if g % 2 == 0 else 3 - p)
                copy(t_pack.at[pl.ds(8 * g, 8), at], t_ref.at[own_t, at], ("ts", cols, g), (to, q), ("ts", cols)).wait_send()


def gather(matrix, index, order, slot_hot, put, lower_inverse, upper_inverse):
    vmem = pl.BlockSpec(memory_space=pltpu.VMEM)
    return pl.pallas_call(
        gather_kernel,
        out_shape=[
            jax.ShapeDtypeStruct((256, COLS), F32),
            jax.ShapeDtypeStruct((TROWS, COLS), F32),
            *weights_of(TROWS),
        ],
        in_specs=[pl.BlockSpec(memory_space=pltpu.SMEM), vmem, vmem, vmem, vmem, vmem, pl.BlockSpec(memory_space=pl.ANY)],
        out_specs=[vmem] * 6,
        scratch_shapes=[
            pltpu.VMEM((ROWS, COLS), F32),
            pltpu.VMEM((8 * GROUPS_R, COLS), F32),
            pltpu.VMEM((8 * GROUPS_R, COLS), F32),
            pltpu.VMEM((NB, COLS), F32),
            pltpu.VMEM((2, EXT, NB), F32),
            pltpu.SemaphoreType.DMA((1,)),
            pltpu.SemaphoreType.DMA((COPIES,)),
            pltpu.SemaphoreType.DMA((COPIES,)),
        ],
        compiler_params=pltpu.CompilerParams(collective_id=0, has_side_effects=True, vmem_limit_bytes=48 << 20),
        name="gather_rows",
    )(index, order, slot_hot, put, lower_inverse, upper_inverse, matrix)


def split(x):
    high = x.astype(BF16)
    return high, (x - high.astype(F32)).astype(BF16)


def weigh(e_ref, put_ref, slot_ref, low_ref, up_ref, w_ref, put16_ref, keep_ref, first_ref):
    p, q = lax.axis_index("prow"), lax.axis_index("pcol")
    row, col = iota((NB, NB), 0), iota((NB, NB), 1)
    lower = [jnp.where(row > col, low_ref[t], jnp.where(row == col, 1.0, 0.0)) for t in range(2)]
    upper = [jnp.where(row <= col, up_ref[t], 0.0) for t in range(2)]
    put = put_ref[...]
    top = iota((ROWS, 1), 0) < NB
    at0, at1 = top & (p == 0), top & (p == 1)
    keep = jnp.where(at0 | at1, 0.0, 1.0 - jnp.sum(put, axis=1, keepdims=True))
    keep_ref[...] = jnp.broadcast_to(keep, (ROWS, NB))
    put16_ref[...] = put.astype(BF16)
    pi0, pi1 = slot_ref[:NB], slot_ref[NB:]
    g0, g1 = hp(lower[0], pi0), hp(lower[1], pi1)
    r0, r1 = e_ref[0, ROWS : ROWS + 256], e_ref[1, ROWS : ROWS + 256]
    k0 = hp(r0, upper[0])
    m1 = g1 - hp(hp(g1, k0), g0)
    u01 = hp(g0, r1)
    c0 = keep * e_ref[0, :ROWS] + hp(put, e_ref[0, ROWS + 256 :])
    c1 = keep * e_ref[1, :ROWS] + hp(put, e_ref[1, ROWS + 256 :])
    pis = jnp.where(p == 0, pi0, pi1)
    blank = jnp.zeros((ROWS - NB, NB), F32)
    c0 = jnp.where(at0 | at1, jnp.concatenate([hp(pis, r0), blank], 0), c0)
    c1 = jnp.where(at1, jnp.concatenate([hp(pi1, r1), blank], 0), c1)
    panel0 = hp(c0, upper[0])
    middle = c1 - hp(panel0, u01)
    panel1 = hp(middle, upper[1])
    w = hp(panel0, g0) + hp(panel1, m1)
    blank2 = jnp.zeros((ROWS - NB, 256), F32)
    w = jnp.where(at0 | at1, jnp.concatenate([-jnp.where(p == 0, g0, m1), blank2], 0), w)
    high, low = split(-w)
    w_ref[:, :256] = high
    w_ref[:, 256:512] = high
    w_ref[:, 512:] = low
    u01_tall = jnp.concatenate([u01, blank], 0)
    first0 = jnp.where(at0, c0, panel0)
    first1 = jnp.where(at0, u01_tall, jnp.where(at1, middle, panel1))
    first_ref[...] = jnp.where(q == 0, first0, first1)


def weights_of(trows):
    return [
        jax.ShapeDtypeStruct((ROWS, 768), BF16),
        jax.ShapeDtypeStruct((ROWS, trows), BF16),
        jax.ShapeDtypeStruct((ROWS, NB), F32),
        jax.ShapeDtypeStruct((ROWS, NB), F32),
    ]


WIDTH = 512


def finish_kernel(a_ref, r_ref, t_ref, w_ref, put16_ref, keep_ref, first_ref, o_ref):
    r_high, r_low = split(r_ref[...])
    t_high, t_low = split(t_ref[...])
    dot = functools.partial(jnp.dot, preferred_element_type=F32)
    rows = jnp.concatenate([r_high, r_low, r_high], 0)
    put16 = put16_ref[...]
    moved = dot(put16, t_high) + dot(put16, t_low)
    o_ref[...] = keep_ref[:, :1] * a_ref[...] + (moved + dot(w_ref[...], rows))

    @pl.when((pl.program_id(0) == 0) & (lax.axis_index("pcol") < 2))
    def _():
        o_ref[:, :NB] = first_ref[...]


def finish(matrix, rows, tops, weights):
    trows = tops.shape[0]
    whole = lambda *dims: pl.BlockSpec(dims, lambda i: (0,) * len(dims))
    wide = lambda n: pl.BlockSpec((n, WIDTH), lambda i: (0, i))
    return pl.pallas_call(
        finish_kernel,
        grid=(COLS // WIDTH,),
        out_shape=jax.ShapeDtypeStruct((ROWS, COLS), F32),
        in_specs=[wide(ROWS), wide(256), wide(trows), whole(ROWS, 768), whole(ROWS, trows), whole(ROWS, NB), whole(ROWS, NB)],
        out_specs=wide(ROWS),
        compiler_params=pltpu.CompilerParams(vmem_limit_bytes=48 << 20),
        name=f"finish_{trows}",
    )(matrix, rows, tops, *weights)


def any_pivots(matrix, meta, slot_hot, lower_inverse, upper_inverse):
    p, q = lax.axis_index("prow"), lax.axis_index("pcol")
    src, dest = meta[:2].reshape(256), meta[2:4].reshape(256)
    lines = jnp.arange(ROWS, dtype=I32)
    mine = hot((local_of(src)[:, None] == lines[None, :]) & (owner_of(src) == p)[:, None])
    rows = hp(hp(slot_hot.T, mine), matrix)
    section = (jnp.arange(256) // NB == p)[:, None]
    tops = jnp.where(section, jnp.concatenate([matrix[:NB], matrix[:NB]], 0), 0.0)
    rows, tops = lax.psum((rows, tops), "prow")
    here = (dest >= 0) & (owner_of(dest) == p)
    put = hot((local_of(dest)[None, :] == lines[:, None]) & here[None, :])
    held = jnp.concatenate([matrix[:, :NB], rows[:, :NB], tops[:, :NB]], 0)
    ext = jnp.stack([lax.psum(jnp.where(q == k, held, 0.0), "pcol") for k in range(2)])
    weights = pl.pallas_call(
        weigh,
        out_shape=weights_of(256),
        compiler_params=pltpu.CompilerParams(vmem_limit_bytes=48 << 20),
        name="weigh",
    )(ext, put, slot_hot, lower_inverse, upper_inverse)
    return finish(matrix, rows, tops, weights)


def spread_pivots(matrix, index, order, slot_hot, put, lower_inverse, upper_inverse):
    rows, tops, *weights = gather(matrix, index, order, slot_hot, put, lower_inverse, upper_inverse)
    return finish(matrix, rows, tops, weights)


def shards(matrix, pivots, lower_inverse, upper_inverse):
    fits, meta, index, order, slot_hot, put = plan(pivots)
    return lax.cond(
        fits[0] > 0,
        lambda: spread_pivots(matrix, index, order, slot_hot, put, lower_inverse, upper_inverse),
        lambda: any_pivots(matrix, meta, slot_hot, lower_inverse, upper_inverse),
    )


def solution(mesh):
    placed = (P("prow", "pcol"), P(), P(), P())
    return jax.shard_map(
        shards, mesh=mesh, in_specs=placed, out_specs=P("prow", "pcol"), check_vma=False
    )
```

```python
import functools

import jax
import jax.numpy as jnp
from jax import lax
from jax.experimental import pallas as pl
from jax.experimental.pallas import tpu as pltpu
from jax.sharding import PartitionSpec as P

MESH = pl.DeviceIdType.MESH
NB = 128
ROWS = 512
COLS = 3072
NPROW = 32
REACH_R = 3
REACH_T = 5
GROUPS_R = 2 * REACH_R + 1
GROUPS_T = 2 * REACH_T + 1
TROWS = 8 * GROUPS_T
EXT = ROWS + 256 + TROWS
F32 = jnp.float32
BF16 = jnp.bfloat16
I32 = jnp.int32


def hp(a, b):
    return jnp.dot(a, b, precision=lax.Precision.HIGHEST, preferred_element_type=F32)


def hot(mask):
    return jnp.where(mask, 1.0, 0.0).astype(F32)


def owner_of(row):
    return (row >> 7) & (NPROW - 1)


def local_of(row):
    return ((row >> 12) << 7) + (row & (NB - 1))


def wrapped(distance):
    return ((distance + 16) & (NPROW - 1)) - 16


def iota(shape, dim):
    return lax.broadcasted_iota(I32, shape, dim)


def both(row):
    n = row.shape[1]
    eye = iota((n, n), 0) == iota((n, n), 1)
    return row, jnp.sum(jnp.where(eye, row, 0), axis=1, keepdims=True)


def ranked(row, col):
    n = row.shape[1]
    key_row, key_col = row * n + iota((1, n), 1), col * n + iota((n, 1), 0)
    in_row = jnp.sum(jnp.where(key_col < key_row, 1, 0), axis=0, keepdims=True)
    in_col = jnp.sum(jnp.where(key_row < key_col, 1, 0), axis=1, keepdims=True)
    return in_row, in_col


def plan_kernel(piv_ref, fits_ref, meta_ref, index_ref, order_ref, slot_ref, put_ref):
    p = lax.axis_index("prow")
    r0, r1 = piv_ref[0:1, :], piv_ref[1:2, :]
    c0 = both(r0)[1]
    line, lane = iota((NB, NB), 0), iota((NB, NB), 1)
    same = c0 == r1
    onto = c0 - NB == lane
    same_i, onto_i = jnp.where(same, 1, 0), jnp.where(onto, 1, 0)
    src1 = jnp.where(jnp.max(same_i, axis=0, keepdims=True) > 0, jnp.sum(same_i * line, axis=0, keepdims=True), r1)
    via = jnp.sum(jnp.where(onto, r1, 0), axis=1, keepdims=True)
    dest0_col = jnp.where(c0 < 2 * NB, via, jnp.where(jnp.max(same_i, axis=1, keepdims=True) > 0, -1, c0))
    dest0 = jnp.sum(jnp.where(line == lane, dest0_col, 0), axis=0, keepdims=True)
    dest1, dest1_col = both(jnp.where(jnp.max(onto_i, axis=0, keepdims=True) > 0, -1, r1))
    meta_ref[0:1, :] = r0
    meta_ref[1:2, :] = src1
    meta_ref[2:3, :] = dest0
    meta_ref[3:4, :] = dest1
    meta_ref[4:8, :] = jnp.zeros((4, NB), I32)

    src, src_col = jnp.concatenate([r0, src1], 1), jnp.concatenate([c0, both(src1)[1]], 0)
    own, own_col = owner_of(src), owner_of(src_col)
    rank, rank_col = ranked(own, own_col)
    skew = 16 * own + 7 - 2 * rank
    turn = (jnp.max(skew, axis=1, keepdims=True) + jnp.min(skew, axis=1, keepdims=True)) >> 2
    slot, slot_col = (rank + turn) & 255, (rank_col + turn) & 255
    off_r = jnp.max(jnp.abs(wrapped((slot >> 3) - own)))
    wanted = (8 * (p - REACH_R) + iota((1, NB), 1)) & 255
    mine = (slot_col == wanted) & (own_col == p)
    index_ref[0:1, :] = jnp.sum(jnp.where(mine, local_of(src_col) + 1, 0), axis=0, keepdims=True) - 1
    slot_ref[...] = hot(slot_col == iota((256, 256), 1))

    put = jnp.zeros((ROWS, NB), F32)
    off_t = 0
    for section, (dest, dest_col) in enumerate(((dest0, dest0_col), (dest1, dest1_col))):
        to = jnp.where(dest >= 0, owner_of(dest), iota((1, NB), 1) >> 2)
        to_col = jnp.where(dest_col >= 0, owner_of(dest_col), iota((NB, 1), 0) >> 2)
        rank, rank_col = ranked(to, to_col)
        skew = 8 * to + 3 - 2 * rank
        turn = (jnp.max(skew, axis=1, keepdims=True) + jnp.min(skew, axis=1, keepdims=True)) >> 2
        place, place_col = (rank + turn) & (NB - 1), (rank_col + turn) & (NB - 1)
        home, home_col = (
            (v >> 4) * 4 + jnp.where(((v >> 3) & 1) == 0, section, 3 - section) for v in (place, place_col)
        )
        off_t = jnp.maximum(off_t, jnp.max(jnp.where(dest >= 0, jnp.abs(wrapped(to - home)), 0)))
        column = ((home_col - p + REACH_T) & (NPROW - 1)) * 8 + (place_col & 7)
        here = (dest >= 0) & (to == p)
        into = hot((local_of(dest) == iota((ROWS, NB), 0)) & here)
        put = put + jnp.dot(into, hot(column == lane), preferred_element_type=F32)

        @pl.when((p == section) | (section == 1) & (p > 1))
        def _():
            order_ref[...] = hot(place == line)

    put_ref[...] = put[:, :TROWS]
    fits_ref[0] = jnp.where((off_r <= REACH_R) & (off_t <= REACH_T), 1, 0)


def plan(pivots):
    vmem = pl.BlockSpec(memory_space=pltpu.VMEM)
    return pl.pallas_call(
        plan_kernel,
        out_shape=[
            jax.ShapeDtypeStruct((1,), I32),
            jax.ShapeDtypeStruct((8, NB), I32),
            jax.ShapeDtypeStruct((1, NB), I32),
            jax.ShapeDtypeStruct((NB, NB), F32),
            jax.ShapeDtypeStruct((256, 256), F32),
            jax.ShapeDtypeStruct((ROWS, TROWS), F32),
        ],
        in_specs=[vmem],
        out_specs=[pl.BlockSpec(memory_space=pltpu.SMEM), vmem, vmem, vmem, vmem, vmem],
        name="plan",
    )(pivots.reshape(2, NB))


A_CHUNKS = ((0, 128, 1), (128, 512, -1), (640, 640, 1))
B_CHUNKS = ((1280, 896, 1), (2176, 896, -1))
SHIFTS = ((0, 128), (1280, 1792), (128, 1152))
T_CHUNKS = ((0, 128), (128, 2944))
COPIES = 224


def hops(long, way):
    return 4 if long == way else 3


def gather_kernel(
    index_ref, order_ref, slot_ref, put_ref, low_ref, up_ref, a_hbm,
    r_ref, t_ref, w_ref, put16_ref, keep_ref, first_ref,
    a_ref, pack, inbox, t_pack, e_ref, load_sem, send_sem, recv_sem,
):
    p, q = lax.axis_index("prow"), lax.axis_index("pcol")
    z, x = lax.div(p, 4), lax.rem(p, 4)
    y, core = lax.div(q, 2), lax.rem(q, 2)
    source = p < 2
    sends, receipts = {}, {}
    pending = []

    def number(numbers, tag):
        assert len(numbers) < COPIES or tag in numbers
        return numbers.setdefault(tag, len(numbers))

    def copy(src, dst, tag, device, recv_tag=None):
        return pltpu.make_async_remote_copy(
            src_ref=src,
            dst_ref=dst,
            send_sem=send_sem.at[number(sends, tag)],
            recv_sem=recv_sem.at[number(receipts, recv_tag or tag)],
            device_id=device,
            device_id_type=MESH,
        )

    def send(src, dst, tag, device):
        c = copy(src, dst, tag, device)
        c.start()
        pending.append(c)

    def arrived(dst, tag):
        copy(dst, dst, tag, core_peer).wait_recv()

    def along(step):
        return lax.rem(p + step + NPROW, NPROW), q

    def at_z(step):
        return lax.rem(z + step + 8, 8) * 4 + x, q

    def at_x(step):
        return z * 4 + lax.rem(x + step + 4, 4), q

    core_peer = (p, y * 2 + 1 - core)

    def block(zz, xx, cols):
        start = pl.multiple_of((lax.rem(z + zz + 8, 8) * 4 + lax.rem(x + xx + 4, 4)) * 8, 8)
        return r_ref.at[pl.ds(start, 8), pl.ds(cols[0], cols[1])]

    def plane(zz, cols):
        start = pl.multiple_of(lax.rem(z + zz + 8, 8) * 32, 32)
        return r_ref.at[pl.ds(start, 32), pl.ds(cols[0], cols[1])]

    load = pltpu.make_async_copy(a_hbm, a_ref, load_sem.at[0])
    load.start()

    barrier = pltpu.get_barrier_semaphore()

    def greet(device):
        pl.semaphore_signal(barrier, inc=1, device_id=device, device_id_type=MESH)

    for step in range(-REACH_T, REACH_T + 1):
        if step:
            greet(along(step))
    greet(core_peer)

    @pl.when(y > 0)
    def _():
        greet((p, core))

    from_row = jnp.where((x == 0) | (x == 3), 0, 1)

    @pl.when(p != from_row)
    def _():
        greet((from_row, q))

    load.wait()

    def take(m, carry):
        r = index_ref[0, m]
        row = a_ref[pl.ds(jnp.maximum(r, 0), 1), :]
        pack[pl.ds(m, 1), :] = jnp.where(r >= 0, row, 0.0)
        return carry

    lax.fori_loop(0, 8 * GROUPS_R, take, 0)
    pl.semaphore_wait(barrier, 2 * REACH_T + 1 + jnp.where(y == 0, 3, 0) + jnp.where(source, 15, 0))

    def shift(cols):
        at = pl.ds(*cols)
        for d in range(-REACH_R, REACH_R + 1):
            if d:
                send(pack.at[pl.ds(8 * (d + REACH_R), 8), at], inbox.at[pl.ds(8 * (REACH_R - d), 8), at], ("shift", cols, d), along(d))

    def settle(cols):
        at = pl.ds(*cols)
        for d in range(-REACH_R, REACH_R + 1):
            if d:
                arrived(inbox.at[pl.ds(8 * (REACH_R - d), 8), at], ("shift", cols, d))
        total = pack[8 * REACH_R : 8 * REACH_R + 8, at]
        for d in range(-REACH_R, REACH_R + 1):
            if d:
                total = total + inbox[8 * (REACH_R - d) : 8 * (REACH_R - d) + 8, at]
        r_ref[pl.ds(pl.multiple_of(p * 8, 8), 8), at] = total

    ext_a = e_ref.at[core, pl.ds(0, ROWS)]
    ext_rt = e_ref.at[core, pl.ds(ROWS, EXT - ROWS)]
    far_a = e_ref.at[1 - core, pl.ds(0, ROWS)]
    far_rt = e_ref.at[1 - core, pl.ds(ROWS, EXT - ROWS)]

    shift(SHIFTS[0])

    @pl.when(y == 0)
    def _():
        e_ref[core, :ROWS] = a_ref[:, :NB]
        for step in (1, 3, 2):
            copy(ext_a, ext_a, ("ya", step), (p, step * 2 + core), ("ya",)).start()

    shift(SHIFTS[1])
    shift(SHIFTS[2])

    own_t = pl.ds(8 * REACH_T, 8)

    @pl.when(source)
    def _():
        def turn(n, carry):
            at = pl.ds(pl.multiple_of(n * 512, 512), 512)
            t_pack[:, at] = hp(order_ref[...], a_ref[:NB, at])
            return carry

        lax.fori_loop(0, COLS // 512, turn, 0)
        for cols in T_CHUNKS:
            at = pl.ds(*cols)
            for g in range(1, 16):
                to = g // 2 * 4 + (p if g % 2 == 0 else 3 - p)
                copy(t_pack.at[pl.ds(8 * g, 8), at], t_ref.at[own_t, at], ("ts", cols, g), (to, q), ("ts", cols)).start()
        t_ref[own_t, :] = t_pack[:8]

    def spread_x(cols):
        for dx in (1, 3, 2):
            send(block(0, 0, cols), block(0, 0, cols), ("a1", cols, dx), at_x(dx))

    def joined_x(cols):
        for dx in (1, 3, 2):
            arrived(block(0, -dx, cols), ("a1", cols, dx))

    def pass_plane(cols, s):
        for way in (1, -1):
            if s > 0:
                if s > hops(cols[2], way):
                    continue
                arrived(plane(-way * s, cols), ("a2", cols, way, s))
            if s < hops(cols[2], way):
                part = plane(-way * s, cols)
                send(part, part, ("a2", cols, way, s + 1), at_z(way))

    def ways_at(cols, s):
        return [0] if s == 0 else [-way * s for way in (1, -1) if s <= hops(cols[2], way)]

    def pass_block(cols, s):
        for way in (1, -1):
            if s > 0:
                if s > hops(cols[2], way):
                    continue
                arrived(block(-way * s, 0, cols), ("b1", cols, way, s))
            part = block(-way * s, 0, cols)
            if s < hops(cols[2], way):
                send(part, part, ("b1", cols, way, s + 1), at_z(way))
            if s > 0 or way == 1:
                for dx in (1, -1):
                    send(part, part, ("b2", cols, -way * s if s else 0, dx), at_x(dx))

    def relay_x(cols, s):
        for zz in ways_at(cols, s):
            for dx in (1, -1):
                arrived(block(zz, -dx, cols), ("b2", cols, zz, dx))
                if dx == cols[2]:
                    part = block(zz, -dx, cols)
                    send(part, part, ("b3", cols, zz), at_x(dx))

    def end_x(cols, s):
        for zz in ways_at(cols, s):
            arrived(block(zz, 2, cols), ("b3", cols, zz))

    def t_ready(cols):
        at = pl.ds(*cols)

        @pl.when(jnp.logical_not(source))
        def _():
            arrived(t_ref.at[own_t, at], ("ts", cols))

        for e in range(-REACH_T, REACH_T + 1):
            if e:
                send(t_ref.at[own_t, at], t_ref.at[pl.ds(8 * (REACH_T - e), 8), at], ("th", cols, e), along(e))

    def t_done(cols):
        at = pl.ds(*cols)
        for e in range(-REACH_T, REACH_T + 1):
            if e:
                arrived(t_ref.at[pl.ds(8 * (REACH_T - e), 8), at], ("th", cols, e))

    first, *rest = A_CHUNKS
    settle(SHIFTS[0])
    spread_x(first)
    settle(SHIFTS[1])
    for cols in B_CHUNKS:
        pass_block(cols, 0)
    settle(SHIFTS[2])
    for cols in rest:
        spread_x(cols)
    joined_x(first)
    pass_plane(first, 0)
    t_ready(T_CHUNKS[0])
    for cols in rest:
        joined_x(cols)
        pass_plane(cols, 0)
    for s in range(1, 5):
        pass_plane(first, s)
        for cols in B_CHUNKS:
            pass_block(cols, s)
        for cols in rest:
            pass_plane(cols, s)
        for cols in B_CHUNKS:
            relay_x(cols, s - 1)
        if s == 4:
            t_ready(T_CHUNKS[1])
    t_done(T_CHUNKS[0])

    @pl.when(y == 0)
    def _():
        e_ref[core, ROWS : ROWS + 256] = r_ref[:, :NB]
        e_ref[core, ROWS + 256 :] = t_ref[:, :NB]
        for step in (1, 3, 2):
            copy(ext_rt, ext_rt, ("yr", step), (p, step * 2 + core), ("yr",)).start()

    @pl.when(y > 0)
    def _():
        arrived(ext_a, ("ya",))

    send(ext_a, ext_a, ("ca",), core_peer)
    for cols in B_CHUNKS:
        relay_x(cols, 4)

    @pl.when(y > 0)
    def _():
        arrived(ext_rt, ("yr",))

    send(ext_rt, ext_rt, ("cr",), core_peer)
    arrived(far_a, ("ca",))
    arrived(far_rt, ("cr",))
    weigh(e_ref, put_ref, slot_ref, low_ref, up_ref, w_ref, put16_ref, keep_ref, first_ref)
    for s in range(5):
        for cols in B_CHUNKS:
            end_x(cols, s)
    t_done(T_CHUNKS[1])
    for c in pending:
        c.wait_send()

    @pl.when(y == 0)
    def _():
        for step in (1, 3, 2):
            copy(ext_a, ext_a, ("ya", step), (p, step * 2 + core), ("ya",)).wait_send()
            copy(ext_rt, ext_rt, ("yr", step), (p, step * 2 + core), ("yr",)).wait_send()

    @pl.when(source)
    def _():
        for cols in T_CHUNKS:
            at = pl.ds(*cols)
            for g in range(1, 16):
                to = g // 2 * 4 + (p if g % 2 == 0 else 3 - p)
                copy(t_pack.at[pl.ds(8 * g, 8), at], t_ref.at[own_t, at], ("ts", cols, g), (to, q), ("ts", cols)).wait_send()


def gather(matrix, index, order, slot_hot, put, lower_inverse, upper_inverse):
    vmem = pl.BlockSpec(memory_space=pltpu.VMEM)
    return pl.pallas_call(
        gather_kernel,
        out_shape=[
            jax.ShapeDtypeStruct((256, COLS), F32),
            jax.ShapeDtypeStruct((TROWS, COLS), F32),
            *weights_of(TROWS),
        ],
        in_specs=[pl.BlockSpec(memory_space=pltpu.SMEM), vmem, vmem, vmem, vmem, vmem, pl.BlockSpec(memory_space=pl.ANY)],
        out_specs=[vmem] * 6,
        scratch_shapes=[
            pltpu.VMEM((ROWS, COLS), F32),
            pltpu.VMEM((8 * GROUPS_R, COLS), F32),
            pltpu.VMEM((8 * GROUPS_R, COLS), F32),
            pltpu.VMEM((NB, COLS), F32),
            pltpu.VMEM((2, EXT, NB), F32),
            pltpu.SemaphoreType.DMA((1,)),
            pltpu.SemaphoreType.DMA((COPIES,)),
            pltpu.SemaphoreType.DMA((COPIES,)),
        ],
        compiler_params=pltpu.CompilerParams(collective_id=0, has_side_effects=True, vmem_limit_bytes=48 << 20),
        name="gather_rows",
    )(index, order, slot_hot, put, lower_inverse, upper_inverse, matrix)


def split(x):
    high = x.astype(BF16)
    return high, (x - high.astype(F32)).astype(BF16)


def weigh(e_ref, put_ref, slot_ref, low_ref, up_ref, w_ref, put16_ref, keep_ref, first_ref):
    p, q = lax.axis_index("prow"), lax.axis_index("pcol")
    row, col = iota((NB, NB), 0), iota((NB, NB), 1)
    lower = [jnp.where(row > col, low_ref[t], jnp.where(row == col, 1.0, 0.0)) for t in range(2)]
    upper = [jnp.where(row <= col, up_ref[t], 0.0) for t in range(2)]
    put = put_ref[...]
    top = iota((ROWS, 1), 0) < NB
    at0, at1 = top & (p == 0), top & (p == 1)
    keep = jnp.where(at0 | at1, 0.0, 1.0 - jnp.sum(put, axis=1, keepdims=True))
    keep_ref[...] = jnp.broadcast_to(keep, (ROWS, NB))
    put16_ref[...] = put.astype(BF16)
    pi0, pi1 = slot_ref[:NB], slot_ref[NB:]
    g0, g1 = hp(lower[0], pi0), hp(lower[1], pi1)
    r0, r1 = e_ref[0, ROWS : ROWS + 256], e_ref[1, ROWS : ROWS + 256]
    k0 = hp(r0, upper[0])
    m1 = g1 - hp(hp(g1, k0), g0)
    u01 = hp(g0, r1)
    c0 = keep * e_ref[0, :ROWS] + hp(put, e_ref[0, ROWS + 256 :])
    c1 = keep * e_ref[1, :ROWS] + hp(put, e_ref[1, ROWS + 256 :])
    pis = jnp.where(p == 0, pi0, pi1)
    blank = jnp.zeros((ROWS - NB, NB), F32)
    c0 = jnp.where(at0 | at1, jnp.concatenate([hp(pis, r0), blank], 0), c0)
    c1 = jnp.where(at1, jnp.concatenate([hp(pi1, r1), blank], 0), c1)
    panel0 = hp(c0, upper[0])
    middle = c1 - hp(panel0, u01)
    panel1 = hp(middle, upper[1])
    w = hp(panel0, g0) + hp(panel1, m1)
    blank2 = jnp.zeros((ROWS - NB, 256), F32)
    w = jnp.where(at0 | at1, jnp.concatenate([-jnp.where(p == 0, g0, m1), blank2], 0), w)
    high, low = split(-w)
    w_ref[:, :256] = high
    w_ref[:, 256:512] = high
    w_ref[:, 512:] = low
    u01_tall = jnp.concatenate([u01, blank], 0)
    first0 = jnp.where(at0, c0, panel0)
    first1 = jnp.where(at0, u01_tall, jnp.where(at1, middle, panel1))
    first_ref[...] = jnp.where(q == 0, first0, first1)


def weights_of(trows):
    return [
        jax.ShapeDtypeStruct((ROWS, 768), BF16),
        jax.ShapeDtypeStruct((ROWS, trows), BF16),
        jax.ShapeDtypeStruct((ROWS, NB), F32),
        jax.ShapeDtypeStruct((ROWS, NB), F32),
    ]


WIDTH = 512


def finish_kernel(a_ref, r_ref, t_ref, w_ref, put16_ref, keep_ref, first_ref, o_ref):
    r_high, r_low = split(r_ref[...])
    t_high, t_low = split(t_ref[...])
    dot = functools.partial(jnp.dot, preferred_element_type=F32)
    rows = jnp.concatenate([r_high, r_low, r_high], 0)
    put16 = put16_ref[...]
    moved = dot(put16, t_high) + dot(put16, t_low)
    o_ref[...] = keep_ref[:, :1] * a_ref[...] + (moved + dot(w_ref[...], rows))

    @pl.when((pl.program_id(0) == 0) & (lax.axis_index("pcol") < 2))
    def _():
        o_ref[:, :NB] = first_ref[...]


def finish(matrix, rows, tops, weights):
    trows = tops.shape[0]
    whole = lambda *dims: pl.BlockSpec(dims, lambda i: (0,) * len(dims))
    wide = lambda n: pl.BlockSpec((n, WIDTH), lambda i: (0, i))
    return pl.pallas_call(
        finish_kernel,
        grid=(COLS // WIDTH,),
        out_shape=jax.ShapeDtypeStruct((ROWS, COLS), F32),
        in_specs=[wide(ROWS), wide(256), wide(trows), whole(ROWS, 768), whole(ROWS, trows), whole(ROWS, NB), whole(ROWS, NB)],
        out_specs=wide(ROWS),
        compiler_params=pltpu.CompilerParams(vmem_limit_bytes=48 << 20),
        name=f"finish_{trows}",
    )(matrix, rows, tops, *weights)


def any_pivots(matrix, meta, slot_hot, lower_inverse, upper_inverse):
    p, q = lax.axis_index("prow"), lax.axis_index("pcol")
    src, dest = meta[:2].reshape(256), meta[2:4].reshape(256)
    lines = jnp.arange(ROWS, dtype=I32)
    mine = hot((local_of(src)[:, None] == lines[None, :]) & (owner_of(src) == p)[:, None])
    rows = hp(hp(slot_hot.T, mine), matrix)
    section = (jnp.arange(256) // NB == p)[:, None]
    tops = jnp.where(section, jnp.concatenate([matrix[:NB], matrix[:NB]], 0), 0.0)
    rows, tops = lax.psum((rows, tops), "prow")
    here = (dest >= 0) & (owner_of(dest) == p)
    put = hot((local_of(dest)[None, :] == lines[:, None]) & here[None, :])
    held = jnp.concatenate([matrix[:, :NB], rows[:, :NB], tops[:, :NB]], 0)
    ext = jnp.stack([lax.psum(jnp.where(q == k, held, 0.0), "pcol") for k in range(2)])
    weights = pl.pallas_call(
        weigh,
        out_shape=weights_of(256),
        compiler_params=pltpu.CompilerParams(vmem_limit_bytes=48 << 20),
        name="weigh",
    )(ext, put, slot_hot, lower_inverse, upper_inverse)
    return finish(matrix, rows, tops, weights)


def spread_pivots(matrix, index, order, slot_hot, put, lower_inverse, upper_inverse):
    rows, tops, *weights = gather(matrix, index, order, slot_hot, put, lower_inverse, upper_inverse)
    return finish(matrix, rows, tops, weights)


def shards(matrix, pivots, lower_inverse, upper_inverse):
    fits, meta, index, order, slot_hot, put = plan(pivots)
    return lax.cond(
        fits[0] > 0,
        lambda: spread_pivots(matrix, index, order, slot_hot, put, lower_inverse, upper_inverse),
        lambda: any_pivots(matrix, meta, slot_hot, lower_inverse, upper_inverse),
    )


def solution(mesh):
    placed = (P("prow", "pcol"), P(), P(), P())
    return jax.shard_map(
        shards, mesh=mesh, in_specs=placed, out_specs=P("prow", "pcol"), check_vma=False
    )
```

```python
import functools

import jax
import jax.numpy as jnp
from jax import lax
from jax.experimental import pallas as pl
from jax.experimental.pallas import tpu as pltpu
from jax.sharding import PartitionSpec as P

MESH = pl.DeviceIdType.MESH
NB = 128
ROWS = 512
COLS = 3072
NPROW = 32
REACH_R = 3
REACH_T = 5
GROUPS_R = 2 * REACH_R + 1
GROUPS_T = 2 * REACH_T + 1
TROWS = 8 * GROUPS_T
EXT = ROWS + 256 + TROWS
F32 = jnp.float32
BF16 = jnp.bfloat16
I32 = jnp.int32


def hp(a, b):
    return jnp.dot(a, b, precision=lax.Precision.HIGHEST, preferred_element_type=F32)


def hot(mask):
    return jnp.where(mask, 1.0, 0.0).astype(F32)


def owner_of(row):
    return (row >> 7) & (NPROW - 1)


def local_of(row):
    return ((row >> 12) << 7) + (row & (NB - 1))


def wrapped(distance):
    return ((distance + 16) & (NPROW - 1)) - 16


def iota(shape, dim):
    return lax.broadcasted_iota(I32, shape, dim)


def both(row):
    n = row.shape[1]
    eye = iota((n, n), 0) == iota((n, n), 1)
    return row, jnp.sum(jnp.where(eye, row, 0), axis=1, keepdims=True)


def ranked(row, col):
    n = row.shape[1]
    key_row, key_col = row * n + iota((1, n), 1), col * n + iota((n, 1), 0)
    in_row = jnp.sum(jnp.where(key_col < key_row, 1, 0), axis=0, keepdims=True)
    in_col = jnp.sum(jnp.where(key_row < key_col, 1, 0), axis=1, keepdims=True)
    return in_row, in_col


def plan_kernel(piv_ref, fits_ref, meta_ref, index_ref, order_ref, slot_ref, put_ref):
    p = lax.axis_index("prow")
    r0, r1 = piv_ref[0:1, :], piv_ref[1:2, :]
    c0 = both(r0)[1]
    line, lane = iota((NB, NB), 0), iota((NB, NB), 1)
    same = c0 == r1
    onto = c0 - NB == lane
    same_i, onto_i = jnp.where(same, 1, 0), jnp.where(onto, 1, 0)
    src1 = jnp.where(jnp.max(same_i, axis=0, keepdims=True) > 0, jnp.sum(same_i * line, axis=0, keepdims=True), r1)
    via = jnp.sum(jnp.where(onto, r1, 0), axis=1, keepdims=True)
    dest0_col = jnp.where(c0 < 2 * NB, via, jnp.where(jnp.max(same_i, axis=1, keepdims=True) > 0, -1, c0))
    dest0 = jnp.sum(jnp.where(line == lane, dest0_col, 0), axis=0, keepdims=True)
    dest1, dest1_col = both(jnp.where(jnp.max(onto_i, axis=0, keepdims=True) > 0, -1, r1))
    meta_ref[0:1, :] = r0
    meta_ref[1:2, :] = src1
    meta_ref[2:3, :] = dest0
    meta_ref[3:4, :] = dest1
    meta_ref[4:8, :] = jnp.zeros((4, NB), I32)

    src, src_col = jnp.concatenate([r0, src1], 1), jnp.concatenate([c0, both(src1)[1]], 0)
    own, own_col = owner_of(src), owner_of(src_col)
    rank, rank_col = ranked(own, own_col)
    skew = 16 * own + 7 - 2 * rank
    turn = (jnp.max(skew, axis=1, keepdims=True) + jnp.min(skew, axis=1, keepdims=True)) >> 2
    slot, slot_col = (rank + turn) & 255, (rank_col + turn) & 255
    off_r = jnp.max(jnp.abs(wrapped((slot >> 3) - own)))
    wanted = (8 * (p - REACH_R) + iota((1, NB), 1)) & 255
    mine = (slot_col == wanted) & (own_col == p)
    index_ref[0:1, :] = jnp.sum(jnp.where(mine, local_of(src_col) + 1, 0), axis=0, keepdims=True) - 1
    slot_ref[...] = hot(slot_col == iota((256, 256), 1))

    put = jnp.zeros((ROWS, NB), F32)
    off_t = 0
    for section, (dest, dest_col) in enumerate(((dest0, dest0_col), (dest1, dest1_col))):
        to = jnp.where(dest >= 0, owner_of(dest), iota((1, NB), 1) >> 2)
        to_col = jnp.where(dest_col >= 0, owner_of(dest_col), iota((NB, 1), 0) >> 2)
        rank, rank_col = ranked(to, to_col)
        skew = 8 * to + 3 - 2 * rank
        turn = (jnp.max(skew, axis=1, keepdims=True) + jnp.min(skew, axis=1, keepdims=True)) >> 2
        place, place_col = (rank + turn) & (NB - 1), (rank_col + turn) & (NB - 1)
        home, home_col = (
            (v >> 4) * 4 + jnp.where(((v >> 3) & 1) == 0, section, 3 - section) for v in (place, place_col)
        )
        off_t = jnp.maximum(off_t, jnp.max(jnp.where(dest >= 0, jnp.abs(wrapped(to - home)), 0)))
        column = ((home_col - p + REACH_T) & (NPROW - 1)) * 8 + (place_col & 7)
        here = (dest >= 0) & (to == p)
        into = hot((local_of(dest) == iota((ROWS, NB), 0)) & here)
        put = put + jnp.dot(into, hot(column == lane), preferred_element_type=F32)

        @pl.when((p == section) | (section == 1) & (p > 1))
        def _():
            order_ref[...] = hot(place == line)

    put_ref[...] = put[:, :TROWS]
    fits_ref[0] = jnp.where((off_r <= REACH_R) & (off_t <= REACH_T), 1, 0)


def plan(pivots):
    vmem = pl.BlockSpec(memory_space=pltpu.VMEM)
    return pl.pallas_call(
        plan_kernel,
        out_shape=[
            jax.ShapeDtypeStruct((1,), I32),
            jax.ShapeDtypeStruct((8, NB), I32),
            jax.ShapeDtypeStruct((1, NB), I32),
            jax.ShapeDtypeStruct((NB, NB), F32),
            jax.ShapeDtypeStruct((256, 256), F32),
            jax.ShapeDtypeStruct((ROWS, TROWS), F32),
        ],
        in_specs=[vmem],
        out_specs=[pl.BlockSpec(memory_space=pltpu.SMEM), vmem, vmem, vmem, vmem, vmem],
        name="plan",
    )(pivots.reshape(2, NB))


A_CHUNKS = ((0, 128, 1), (128, 512, -1), (640, 640, 1))
B_CHUNKS = ((1280, 896, 1), (2176, 896, -1))
SHIFTS = ((0, 128), (1280, 1792), (128, 1152))
T_CHUNKS = ((0, 128), (128, 2944))
COPIES = 224


def hops(long, way):
    return 4 if long == way else 3


def gather_kernel(
    index_ref, order_ref, slot_ref, put_ref, low_ref, up_ref, a_hbm,
    r_ref, t_ref, w_ref, put16_ref, keep_ref, first_ref,
    a_ref, pack, inbox, t_pack, e_ref, load_sem, send_sem, recv_sem,
):
    p, q = lax.axis_index("prow"), lax.axis_index("pcol")
    z, x = lax.div(p, 4), lax.rem(p, 4)
    y, core = lax.div(q, 2), lax.rem(q, 2)
    source = p < 2
    sends, receipts = {}, {}
    pending = []

    def number(numbers, tag):
        assert len(numbers) < COPIES or tag in numbers
        return numbers.setdefault(tag, len(numbers))

    def copy(src, dst, tag, device, recv_tag=None):
        return pltpu.make_async_remote_copy(
            src_ref=src,
            dst_ref=dst,
            send_sem=send_sem.at[number(sends, tag)],
            recv_sem=recv_sem.at[number(receipts, recv_tag or tag)],
            device_id=device,
            device_id_type=MESH,
        )

    def send(src, dst, tag, device):
        c = copy(src, dst, tag, device)
        c.start()
        pending.append(c)

    def arrived(dst, tag):
        copy(dst, dst, tag, core_peer).wait_recv()

    def along(step):
        return lax.rem(p + step + NPROW, NPROW), q

    def at_z(step):
        return lax.rem(z + step + 8, 8) * 4 + x, q

    def at_x(step):
        return z * 4 + lax.rem(x + step + 4, 4), q

    core_peer = (p, y * 2 + 1 - core)

    def block(zz, xx, cols):
        start = pl.multiple_of((lax.rem(z + zz + 8, 8) * 4 + lax.rem(x + xx + 4, 4)) * 8, 8)
        return r_ref.at[pl.ds(start, 8), pl.ds(cols[0], cols[1])]

    def plane(zz, cols):
        start = pl.multiple_of(lax.rem(z + zz + 8, 8) * 32, 32)
        return r_ref.at[pl.ds(start, 32), pl.ds(cols[0], cols[1])]

    load = pltpu.make_async_copy(a_hbm, a_ref, load_sem.at[0])
    load.start()

    barrier = pltpu.get_barrier_semaphore()

    def greet(device):
        pl.semaphore_signal(barrier, inc=1, device_id=device, device_id_type=MESH)

    for step in range(-REACH_T, REACH_T + 1):
        if step:
            greet(along(step))
    greet(core_peer)

    @pl.when(y > 0)
    def _():
        greet((p, core))

    from_row = jnp.where((x == 0) | (x == 3), 0, 1)

    @pl.when(p != from_row)
    def _():
        greet((from_row, q))

    load.wait()

    def take(m, carry):
        r = index_ref[0, m]
        row = a_ref[pl.ds(jnp.maximum(r, 0), 1), :]
        pack[pl.ds(m, 1), :] = jnp.where(r >= 0, row, 0.0)
        return carry

    lax.fori_loop(0, 8 * GROUPS_R, take, 0)
    pl.semaphore_wait(barrier, 2 * REACH_T + 1 + jnp.where(y == 0, 3, 0) + jnp.where(source, 15, 0))

    def shift(cols):
        at = pl.ds(*cols)
        for d in range(-REACH_R, REACH_R + 1):
            if d:
                send(pack.at[pl.ds(8 * (d + REACH_R), 8), at], inbox.at[pl.ds(8 * (REACH_R - d), 8), at], ("shift", cols, d), along(d))

    def settle(cols):
        at = pl.ds(*cols)
        for d in range(-REACH_R, REACH_R + 1):
            if d:
                arrived(inbox.at[pl.ds(8 * (REACH_R - d), 8), at], ("shift", cols, d))
        total = pack[8 * REACH_R : 8 * REACH_R + 8, at]
        for d in range(-REACH_R, REACH_R + 1):
            if d:
                total = total + inbox[8 * (REACH_R - d) : 8 * (REACH_R - d) + 8, at]
        r_ref[pl.ds(pl.multiple_of(p * 8, 8), 8), at] = total

    ext_a = e_ref.at[core, pl.ds(0, ROWS)]
    ext_rt = e_ref.at[core, pl.ds(ROWS, EXT - ROWS)]
    far_a = e_ref.at[1 - core, pl.ds(0, ROWS)]
    far_rt = e_ref.at[1 - core, pl.ds(ROWS, EXT - ROWS)]

    shift(SHIFTS[0])

    @pl.when(y == 0)
    def _():
        e_ref[core, :ROWS] = a_ref[:, :NB]
        for step in (1, 3, 2):
            copy(ext_a, ext_a, ("ya", step), (p, step * 2 + core), ("ya",)).start()

    shift(SHIFTS[1])
    shift(SHIFTS[2])

    own_t = pl.ds(8 * REACH_T, 8)

    @pl.when(source)
    def _():
        def turn(n, carry):
            at = pl.ds(pl.multiple_of(n * 512, 512), 512)
            t_pack[:, at] = hp(order_ref[...], a_ref[:NB, at])
            return carry

        lax.fori_loop(0, COLS // 512, turn, 0)
        for cols in T_CHUNKS:
            at = pl.ds(*cols)
            for g in range(1, 16):
                to = g // 2 * 4 + (p if g % 2 == 0 else 3 - p)
                copy(t_pack.at[pl.ds(8 * g, 8), at], t_ref.at[own_t, at], ("ts", cols, g), (to, q), ("ts", cols)).start()
        t_ref[own_t, :] = t_pack[:8]

    def spread_x(cols):
        for dx in (1, 3, 2):
            send(block(0, 0, cols), block(0, 0, cols), ("a1", cols, dx), at_x(dx))

    def joined_x(cols):
        for dx in (1, 3, 2):
            arrived(block(0, -dx, cols), ("a1", cols, dx))

    def pass_plane(cols, s):
        for way in (1, -1):
            if s > 0:
                if s > hops(cols[2], way):
                    continue
                arrived(plane(-way * s, cols), ("a2", cols, way, s))
            if s < hops(cols[2], way):
                part = plane(-way * s, cols)
                send(part, part, ("a2", cols, way, s + 1), at_z(way))

    def ways_at(cols, s):
        return [0] if s == 0 else [-way * s for way in (1, -1) if s <= hops(cols[2], way)]

    def pass_block(cols, s):
        for way in (1, -1):
            if s > 0:
                if s > hops(cols[2], way):
                    continue
                arrived(block(-way * s, 0, cols), ("b1", cols, way, s))
            part = block(-way * s, 0, cols)
            if s < hops(cols[2], way):
                send(part, part, ("b1", cols, way, s + 1), at_z(way))
            if s > 0 or way == 1:
                for dx in (1, -1):
                    send(part, part, ("b2", cols, -way * s if s else 0, dx), at_x(dx))

    def relay_x(cols, s):
        for zz in ways_at(cols, s):
            for dx in (1, -1):
                arrived(block(zz, -dx, cols), ("b2", cols, zz, dx))
                if dx == cols[2]:
                    part = block(zz, -dx, cols)
                    send(part, part, ("b3", cols, zz), at_x(dx))

    def end_x(cols, s):
        for zz in ways_at(cols, s):
            arrived(block(zz, 2, cols), ("b3", cols, zz))

    def t_ready(cols):
        at = pl.ds(*cols)

        @pl.when(jnp.logical_not(source))
        def _():
            arrived(t_ref.at[own_t, at], ("ts", cols))

        for e in range(-REACH_T, REACH_T + 1):
            if e:
                send(t_ref.at[own_t, at], t_ref.at[pl.ds(8 * (REACH_T - e), 8), at], ("th", cols, e), along(e))

    def t_done(cols):
        at = pl.ds(*cols)
        for e in range(-REACH_T, REACH_T + 1):
            if e:
                arrived(t_ref.at[pl.ds(8 * (REACH_T - e), 8), at], ("th", cols, e))

    first, *rest = A_CHUNKS
    settle(SHIFTS[0])
    spread_x(first)
    settle(SHIFTS[1])
    for cols in B_CHUNKS:
        pass_block(cols, 0)
    settle(SHIFTS[2])
    for cols in rest:
        spread_x(cols)
    joined_x(first)
    pass_plane(first, 0)
    t_ready(T_CHUNKS[0])
    for cols in rest:
        joined_x(cols)
        pass_plane(cols, 0)
    for s in range(1, 5):
        pass_plane(first, s)
        for cols in B_CHUNKS:
            pass_block(cols, s)
        for cols in rest:
            pass_plane(cols, s)
        for cols in B_CHUNKS:
            relay_x(cols, s - 1)
        if s == 4:
            t_ready(T_CHUNKS[1])
    t_done(T_CHUNKS[0])

    @pl.when(y == 0)
    def _():
        e_ref[core, ROWS : ROWS + 256] = r_ref[:, :NB]
        e_ref[core, ROWS + 256 :] = t_ref[:, :NB]
        for step in (1, 3, 2):
            copy(ext_rt, ext_rt, ("yr", step), (p, step * 2 + core), ("yr",)).start()

    @pl.when(y > 0)
    def _():
        arrived(ext_a, ("ya",))

    send(ext_a, ext_a, ("ca",), core_peer)
    for cols in B_CHUNKS:
        relay_x(cols, 4)

    @pl.when(y > 0)
    def _():
        arrived(ext_rt, ("yr",))

    send(ext_rt, ext_rt, ("cr",), core_peer)
    arrived(far_a, ("ca",))
    arrived(far_rt, ("cr",))
    weigh(e_ref, put_ref, slot_ref, low_ref, up_ref, w_ref, put16_ref, keep_ref, first_ref)
    for s in range(5):
        for cols in B_CHUNKS:
            end_x(cols, s)
    t_done(T_CHUNKS[1])
    for c in pending:
        c.wait_send()

    @pl.when(y == 0)
    def _():
        for step in (1, 3, 2):
            copy(ext_a, ext_a, ("ya", step), (p, step * 2 + core), ("ya",)).wait_send()
            copy(ext_rt, ext_rt, ("yr", step), (p, step * 2 + core), ("yr",)).wait_send()

    @pl.when(source)
    def _():
        for cols in T_CHUNKS:
            at = pl.ds(*cols)
            for g in range(1, 16):
                to = g // 2 * 4 + (p if g % 2 == 0 else 3 - p)
                copy(t_pack.at[pl.ds(8 * g, 8), at], t_ref.at[own_t, at], ("ts", cols, g), (to, q), ("ts", cols)).wait_send()


def gather(matrix, index, order, slot_hot, put, lower_inverse, upper_inverse):
    vmem = pl.BlockSpec(memory_space=pltpu.VMEM)
    return pl.pallas_call(
        gather_kernel,
        out_shape=[
            jax.ShapeDtypeStruct((256, COLS), F32),
            jax.ShapeDtypeStruct((TROWS, COLS), F32),
            *weights_of(TROWS),
        ],
        in_specs=[pl.BlockSpec(memory_space=pltpu.SMEM), vmem, vmem, vmem, vmem, vmem, pl.BlockSpec(memory_space=pl.ANY)],
        out_specs=[vmem] * 6,
        scratch_shapes=[
            pltpu.VMEM((ROWS, COLS), F32),
            pltpu.VMEM((8 * GROUPS_R, COLS), F32),
            pltpu.VMEM((8 * GROUPS_R, COLS), F32),
            pltpu.VMEM((NB, COLS), F32),
            pltpu.VMEM((2, EXT, NB), F32),
            pltpu.SemaphoreType.DMA((1,)),
            pltpu.SemaphoreType.DMA((COPIES,)),
            pltpu.SemaphoreType.DMA((COPIES,)),
        ],
        compiler_params=pltpu.CompilerParams(collective_id=0, has_side_effects=True, vmem_limit_bytes=48 << 20),
        name="gather_rows",
    )(index, order, slot_hot, put, lower_inverse, upper_inverse, matrix)


def split(x):
    high = x.astype(BF16)
    return high, (x - high.astype(F32)).astype(BF16)


def weigh(e_ref, put_ref, slot_ref, low_ref, up_ref, w_ref, put16_ref, keep_ref, first_ref):
    p, q = lax.axis_index("prow"), lax.axis_index("pcol")
    row, col = iota((NB, NB), 0), iota((NB, NB), 1)
    lower = [jnp.where(row > col, low_ref[t], jnp.where(row == col, 1.0, 0.0)) for t in range(2)]
    upper = [jnp.where(row <= col, up_ref[t], 0.0) for t in range(2)]
    put = put_ref[...]
    top = iota((ROWS, 1), 0) < NB
    at0, at1 = top & (p == 0), top & (p == 1)
    keep = jnp.where(at0 | at1, 0.0, 1.0 - jnp.sum(put, axis=1, keepdims=True))
    keep_ref[...] = jnp.broadcast_to(keep, (ROWS, NB))
    put16_ref[...] = put.astype(BF16)
    pi0, pi1 = slot_ref[:NB], slot_ref[NB:]
    g0, g1 = hp(lower[0], pi0), hp(lower[1], pi1)
    r0, r1 = e_ref[0, ROWS : ROWS + 256], e_ref[1, ROWS : ROWS + 256]
    k0 = hp(r0, upper[0])
    m1 = g1 - hp(hp(g1, k0), g0)
    u01 = hp(g0, r1)
    c0 = keep * e_ref[0, :ROWS] + hp(put, e_ref[0, ROWS + 256 :])
    c1 = keep * e_ref[1, :ROWS] + hp(put, e_ref[1, ROWS + 256 :])
    pis = jnp.where(p == 0, pi0, pi1)
    blank = jnp.zeros((ROWS - NB, NB), F32)
    c0 = jnp.where(at0 | at1, jnp.concatenate([hp(pis, r0), blank], 0), c0)
    c1 = jnp.where(at1, jnp.concatenate([hp(pi1, r1), blank], 0), c1)
    panel0 = hp(c0, upper[0])
    middle = c1 - hp(panel0, u01)
    panel1 = hp(middle, upper[1])
    w = hp(panel0, g0) + hp(panel1, m1)
    blank2 = jnp.zeros((ROWS - NB, 256), F32)
    w = jnp.where(at0 | at1, jnp.concatenate([-jnp.where(p == 0, g0, m1), blank2], 0), w)
    high, low = split(-w)
    w_ref[:, :256] = high
    w_ref[:, 256:512] = high
    w_ref[:, 512:] = low
    u01_tall = jnp.concatenate([u01, blank], 0)
    first0 = jnp.where(at0, c0, panel0)
    first1 = jnp.where(at0, u01_tall, jnp.where(at1, middle, panel1))
    first_ref[...] = jnp.where(q == 0, first0, first1)


def weights_of(trows):
    return [
        jax.ShapeDtypeStruct((ROWS, 768), BF16),
        jax.ShapeDtypeStruct((ROWS, trows), BF16),
        jax.ShapeDtypeStruct((ROWS, NB), F32),
        jax.ShapeDtypeStruct((ROWS, NB), F32),
    ]


WIDTH = 768


def finish_kernel(a_ref, r_ref, t_ref, w_ref, put16_ref, keep_ref, first_ref, o_ref):
    r_high, r_low = split(r_ref[...])
    t_high, t_low = split(t_ref[...])
    dot = functools.partial(jnp.dot, preferred_element_type=F32)
    rows = jnp.concatenate([r_high, r_low, r_high], 0)
    put16 = put16_ref[...]
    moved = dot(put16, t_high) + dot(put16, t_low)
    o_ref[...] = keep_ref[:, :1] * a_ref[...] + (moved + dot(w_ref[...], rows))

    @pl.when((pl.program_id(0) == 0) & (lax.axis_index("pcol") < 2))
    def _():
        o_ref[:, :NB] = first_ref[...]


def finish(matrix, rows, tops, weights):
    trows = tops.shape[0]
    whole = lambda *dims: pl.BlockSpec(dims, lambda i: (0,) * len(dims))
    wide = lambda n: pl.BlockSpec((n, WIDTH), lambda i: (0, i))
    return pl.pallas_call(
        finish_kernel,
        grid=(COLS // WIDTH,),
        out_shape=jax.ShapeDtypeStruct((ROWS, COLS), F32),
        in_specs=[wide(ROWS), wide(256), wide(trows), whole(ROWS, 768), whole(ROWS, trows), whole(ROWS, NB), whole(ROWS, NB)],
        out_specs=wide(ROWS),
        compiler_params=pltpu.CompilerParams(vmem_limit_bytes=48 << 20),
        name=f"finish_{trows}",
    )(matrix, rows, tops, *weights)


def any_pivots(matrix, meta, slot_hot, lower_inverse, upper_inverse):
    p, q = lax.axis_index("prow"), lax.axis_index("pcol")
    src, dest = meta[:2].reshape(256), meta[2:4].reshape(256)
    lines = jnp.arange(ROWS, dtype=I32)
    mine = hot((local_of(src)[:, None] == lines[None, :]) & (owner_of(src) == p)[:, None])
    rows = hp(hp(slot_hot.T, mine), matrix)
    section = (jnp.arange(256) // NB == p)[:, None]
    tops = jnp.where(section, jnp.concatenate([matrix[:NB], matrix[:NB]], 0), 0.0)
    rows, tops = lax.psum((rows, tops), "prow")
    here = (dest >= 0) & (owner_of(dest) == p)
    put = hot((local_of(dest)[None, :] == lines[:, None]) & here[None, :])
    held = jnp.concatenate([matrix[:, :NB], rows[:, :NB], tops[:, :NB]], 0)
    ext = jnp.stack([lax.psum(jnp.where(q == k, held, 0.0), "pcol") for k in range(2)])
    weights = pl.pallas_call(
        weigh,
        out_shape=weights_of(256),
        compiler_params=pltpu.CompilerParams(vmem_limit_bytes=48 << 20),
        name="weigh",
    )(ext, put, slot_hot, lower_inverse, upper_inverse)
    return finish(matrix, rows, tops, weights)


def spread_pivots(matrix, index, order, slot_hot, put, lower_inverse, upper_inverse):
    rows, tops, *weights = gather(matrix, index, order, slot_hot, put, lower_inverse, upper_inverse)
    return finish(matrix, rows, tops, weights)


def shards(matrix, pivots, lower_inverse, upper_inverse):
    fits, meta, index, order, slot_hot, put = plan(pivots)
    return lax.cond(
        fits[0] > 0,
        lambda: spread_pivots(matrix, index, order, slot_hot, put, lower_inverse, upper_inverse),
        lambda: any_pivots(matrix, meta, slot_hot, lower_inverse, upper_inverse),
    )


def solution(mesh):
    placed = (P("prow", "pcol"), P(), P(), P())
    return jax.shard_map(
        shards, mesh=mesh, in_specs=placed, out_specs=P("prow", "pcol"), check_vma=False
    )
```

```python
import functools

import jax
import jax.numpy as jnp
from jax import lax
from jax.experimental import pallas as pl
from jax.experimental.pallas import tpu as pltpu
from jax.sharding import PartitionSpec as P

MESH = pl.DeviceIdType.MESH
NB = 128
ROWS = 512
COLS = 3072
NPROW = 32
REACH_R = 3
REACH_T = 5
GROUPS_R = 2 * REACH_R + 1
GROUPS_T = 2 * REACH_T + 1
TROWS = 8 * GROUPS_T
EXT = ROWS + 256 + TROWS
F32 = jnp.float32
BF16 = jnp.bfloat16
I32 = jnp.int32


def hp(a, b):
    return jnp.dot(a, b, precision=lax.Precision.HIGHEST, preferred_element_type=F32)


def hot(mask):
    return jnp.where(mask, 1.0, 0.0).astype(F32)


def owner_of(row):
    return (row >> 7) & (NPROW - 1)


def local_of(row):
    return ((row >> 12) << 7) + (row & (NB - 1))


def wrapped(distance):
    return ((distance + 16) & (NPROW - 1)) - 16


def iota(shape, dim):
    return lax.broadcasted_iota(I32, shape, dim)


def both(row):
    n = row.shape[1]
    eye = iota((n, n), 0) == iota((n, n), 1)
    return row, jnp.sum(jnp.where(eye, row, 0), axis=1, keepdims=True)


def ranked(row, col):
    n = row.shape[1]
    key_row, key_col = row * n + iota((1, n), 1), col * n + iota((n, 1), 0)
    in_row = jnp.sum(jnp.where(key_col < key_row, 1, 0), axis=0, keepdims=True)
    in_col = jnp.sum(jnp.where(key_row < key_col, 1, 0), axis=1, keepdims=True)
    return in_row, in_col


def plan_kernel(piv_ref, fits_ref, meta_ref, index_ref, order_ref, slot_ref, put_ref):
    p = lax.axis_index("prow")
    r0, r1 = piv_ref[0:1, :], piv_ref[1:2, :]
    c0 = both(r0)[1]
    line, lane = iota((NB, NB), 0), iota((NB, NB), 1)
    same = c0 == r1
    onto = c0 - NB == lane
    same_i, onto_i = jnp.where(same, 1, 0), jnp.where(onto, 1, 0)
    src1 = jnp.where(jnp.max(same_i, axis=0, keepdims=True) > 0, jnp.sum(same_i * line, axis=0, keepdims=True), r1)
    via = jnp.sum(jnp.where(onto, r1, 0), axis=1, keepdims=True)
    dest0_col = jnp.where(c0 < 2 * NB, via, jnp.where(jnp.max(same_i, axis=1, keepdims=True) > 0, -1, c0))
    dest0 = jnp.sum(jnp.where(line == lane, dest0_col, 0), axis=0, keepdims=True)
    dest1, dest1_col = both(jnp.where(jnp.max(onto_i, axis=0, keepdims=True) > 0, -1, r1))
    meta_ref[0:1, :] = r0
    meta_ref[1:2, :] = src1
    meta_ref[2:3, :] = dest0
    meta_ref[3:4, :] = dest1
    meta_ref[4:8, :] = jnp.zeros((4, NB), I32)

    src, src_col = jnp.concatenate([r0, src1], 1), jnp.concatenate([c0, both(src1)[1]], 0)
    own, own_col = owner_of(src), owner_of(src_col)
    rank, rank_col = ranked(own, own_col)
    skew = 16 * own + 7 - 2 * rank
    turn = (jnp.max(skew, axis=1, keepdims=True) + jnp.min(skew, axis=1, keepdims=True)) >> 2
    slot, slot_col = (rank + turn) & 255, (rank_col + turn) & 255
    off_r = jnp.max(jnp.abs(wrapped((slot >> 3) - own)))
    wanted = (8 * (p - REACH_R) + iota((1, NB), 1)) & 255
    mine = (slot_col == wanted) & (own_col == p)
    index_ref[0:1, :] = jnp.sum(jnp.where(mine, local_of(src_col) + 1, 0), axis=0, keepdims=True) - 1
    slot_ref[...] = hot(slot_col == iota((256, 256), 1))

    put = jnp.zeros((ROWS, NB), F32)
    off_t = 0
    for section, (dest, dest_col) in enumerate(((dest0, dest0_col), (dest1, dest1_col))):
        to = jnp.where(dest >= 0, owner_of(dest), iota((1, NB), 1) >> 2)
        to_col = jnp.where(dest_col >= 0, owner_of(dest_col), iota((NB, 1), 0) >> 2)
        rank, rank_col = ranked(to, to_col)
        skew = 8 * to + 3 - 2 * rank
        turn = (jnp.max(skew, axis=1, keepdims=True) + jnp.min(skew, axis=1, keepdims=True)) >> 2
        place, place_col = (rank + turn) & (NB - 1), (rank_col + turn) & (NB - 1)
        home, home_col = (
            (v >> 4) * 4 + jnp.where(((v >> 3) & 1) == 0, section, 3 - section) for v in (place, place_col)
        )
        off_t = jnp.maximum(off_t, jnp.max(jnp.where(dest >= 0, jnp.abs(wrapped(to - home)), 0)))
        column = ((home_col - p + REACH_T) & (NPROW - 1)) * 8 + (place_col & 7)
        here = (dest >= 0) & (to == p)
        into = hot((local_of(dest) == iota((ROWS, NB), 0)) & here)
        put = put + jnp.dot(into, hot(column == lane), preferred_element_type=F32)

        @pl.when((p == section) | (section == 1) & (p > 1))
        def _():
            order_ref[...] = hot(place == line)

    put_ref[...] = put[:, :TROWS]
    fits_ref[0] = jnp.where((off_r <= REACH_R) & (off_t <= REACH_T), 1, 0)


def plan(pivots):
    vmem = pl.BlockSpec(memory_space=pltpu.VMEM)
    return pl.pallas_call(
        plan_kernel,
        out_shape=[
            jax.ShapeDtypeStruct((1,), I32),
            jax.ShapeDtypeStruct((8, NB), I32),
            jax.ShapeDtypeStruct((1, NB), I32),
            jax.ShapeDtypeStruct((NB, NB), F32),
            jax.ShapeDtypeStruct((256, 256), F32),
            jax.ShapeDtypeStruct((ROWS, TROWS), F32),
        ],
        in_specs=[vmem],
        out_specs=[pl.BlockSpec(memory_space=pltpu.SMEM), vmem, vmem, vmem, vmem, vmem],
        name="plan",
    )(pivots.reshape(2, NB))


A_CHUNKS = ((0, 128, 1), (128, 512, -1), (640, 640, 1))
B_CHUNKS = ((1280, 896, 1), (2176, 896, -1))
SHIFTS = ((0, 128), (1280, 1792), (128, 1152))
T_CHUNKS = ((0, 128), (128, 2944))
COPIES = 240
TOPS_AT = (4, 4)
PREPACK = True
GROUP_ORDER = tuple(range(1, 16))


def hops(long, way):
    return 4 if long == way else 3


def gather_kernel(
    index_ref, order_ref, slot_ref, put_ref, low_ref, up_ref, a_hbm,
    r_ref, t_ref, w_ref, put16_ref, keep_ref, first_ref,
    a_ref, pack, inbox, t_pack, e_ref, load_sem, send_sem, recv_sem,
):
    p, q = lax.axis_index("prow"), lax.axis_index("pcol")
    z, x = lax.div(p, 4), lax.rem(p, 4)
    y, core = lax.div(q, 2), lax.rem(q, 2)
    source = p < 2
    sends, receipts = {}, {}
    pending = []

    def number(numbers, tag):
        assert len(numbers) < COPIES or tag in numbers
        return numbers.setdefault(tag, len(numbers))

    def copy(src, dst, tag, device, recv_tag=None):
        return pltpu.make_async_remote_copy(
            src_ref=src,
            dst_ref=dst,
            send_sem=send_sem.at[number(sends, tag)],
            recv_sem=recv_sem.at[number(receipts, recv_tag or tag)],
            device_id=device,
            device_id_type=MESH,
        )

    def send(src, dst, tag, device):
        c = copy(src, dst, tag, device)
        c.start()
        pending.append(c)

    def arrived(dst, tag):
        copy(dst, dst, tag, core_peer).wait_recv()

    def along(step):
        return lax.rem(p + step + NPROW, NPROW), q

    def at_z(step):
        return lax.rem(z + step + 8, 8) * 4 + x, q

    def at_x(step):
        return z * 4 + lax.rem(x + step + 4, 4), q

    core_peer = (p, y * 2 + 1 - core)

    def block(zz, xx, cols):
        start = pl.multiple_of((lax.rem(z + zz + 8, 8) * 4 + lax.rem(x + xx + 4, 4)) * 8, 8)
        return r_ref.at[pl.ds(start, 8), pl.ds(cols[0], cols[1])]

    def plane(zz, cols):
        start = pl.multiple_of(lax.rem(z + zz + 8, 8) * 32, 32)
        return r_ref.at[pl.ds(start, 32), pl.ds(cols[0], cols[1])]

    load = pltpu.make_async_copy(a_hbm, a_ref, load_sem.at[0])
    load.start()

    barrier = pltpu.get_barrier_semaphore()

    def greet(device):
        pl.semaphore_signal(barrier, inc=1, device_id=device, device_id_type=MESH)

    for step in range(-REACH_T, REACH_T + 1):
        if step:
            greet(along(step))
    greet(core_peer)

    @pl.when(y > 0)
    def _():
        greet((p, core))

    from_row = jnp.where((x == 0) | (x == 3), 0, 1)

    @pl.when(p != from_row)
    def _():
        greet((from_row, q))

    load.wait()

    def take(m, carry):
        r = index_ref[0, m]
        row = a_ref[pl.ds(jnp.maximum(r, 0), 1), :]
        pack[pl.ds(m, 1), :] = jnp.where(r >= 0, row, 0.0)
        return carry

    lax.fori_loop(0, 8 * GROUPS_R, take, 0)

    def turn_all():
        order16 = order_ref[...].astype(BF16)

        def turn(n, carry):
            at = pl.ds(pl.multiple_of(n * 512, 512), 512)
            rows = a_ref[:NB, at]
            high = rows.astype(BF16)
            rest = rows - high.astype(F32)
            middle = rest.astype(BF16)
            low = (rest - middle.astype(F32)).astype(BF16)
            dot = functools.partial(jnp.dot, preferred_element_type=F32)
            t_pack[:, at] = dot(order16, high) + (dot(order16, middle) + dot(order16, low))
            return carry

        lax.fori_loop(0, COLS // 512, turn, 0)

    if PREPACK:

        @pl.when(source)
        def _():
            turn_all()

    pl.semaphore_wait(barrier, 2 * REACH_T + 1 + jnp.where(y == 0, 3, 0) + jnp.where(source, 15, 0))

    def shift(cols):
        at = pl.ds(*cols)
        for d in range(-REACH_R, REACH_R + 1):
            if d:
                send(pack.at[pl.ds(8 * (d + REACH_R), 8), at], inbox.at[pl.ds(8 * (REACH_R - d), 8), at], ("shift", cols, d), along(d))

    def settle(cols):
        at = pl.ds(*cols)
        for d in range(-REACH_R, REACH_R + 1):
            if d:
                arrived(inbox.at[pl.ds(8 * (REACH_R - d), 8), at], ("shift", cols, d))
        total = pack[8 * REACH_R : 8 * REACH_R + 8, at]
        for d in range(-REACH_R, REACH_R + 1):
            if d:
                total = total + inbox[8 * (REACH_R - d) : 8 * (REACH_R - d) + 8, at]
        r_ref[pl.ds(pl.multiple_of(p * 8, 8), 8), at] = total

    ext_a = e_ref.at[core, pl.ds(0, ROWS)]
    ext_rt = e_ref.at[core, pl.ds(ROWS, EXT - ROWS)]
    far_a = e_ref.at[1 - core, pl.ds(0, ROWS)]
    far_rt = e_ref.at[1 - core, pl.ds(ROWS, EXT - ROWS)]

    shift(SHIFTS[0])

    @pl.when(y == 0)
    def _():
        e_ref[core, :ROWS] = a_ref[:, :NB]
        for step in (1, 3, 2):
            copy(ext_a, ext_a, ("ya", step), (p, step * 2 + core), ("ya",)).start()

    shift(SHIFTS[1])
    shift(SHIFTS[2])

    own_t = pl.ds(8 * REACH_T, 8)

    @pl.when(source)
    def _():
        if not PREPACK:
            turn_all()
        for cols in T_CHUNKS:
            at = pl.ds(*cols)
            for g in GROUP_ORDER:
                to = g // 2 * 4 + (p if g % 2 == 0 else 3 - p)
                copy(t_pack.at[pl.ds(8 * g, 8), at], t_ref.at[own_t, at], ("ts", cols, g), (to, q), ("ts", cols)).start()
        t_ref[own_t, :] = t_pack[:8]

    def spread_x(cols):
        for dx in (1, 3, 2):
            send(block(0, 0, cols), block(0, 0, cols), ("a1", cols, dx), at_x(dx))

    def joined_x(cols):
        for dx in (1, 3, 2):
            arrived(block(0, -dx, cols), ("a1", cols, dx))

    def pass_plane(cols, s):
        for way in (1, -1):
            if s > 0:
                if s > hops(cols[2], way):
                    continue
                arrived(plane(-way * s, cols), ("a2", cols, way, s))
            if s < hops(cols[2], way):
                part = plane(-way * s, cols)
                send(part, part, ("a2", cols, way, s + 1), at_z(way))

    def ways_at(cols, s):
        return [0] if s == 0 else [-way * s for way in (1, -1) if s <= hops(cols[2], way)]

    def pass_block(cols, s):
        for way in (1, -1):
            if s > 0:
                if s > hops(cols[2], way):
                    continue
                arrived(block(-way * s, 0, cols), ("b1", cols, way, s))
            part = block(-way * s, 0, cols)
            if s < hops(cols[2], way):
                send(part, part, ("b1", cols, way, s + 1), at_z(way))
            if s > 0 or way == 1:
                for dx in (1, -1):
                    send(part, part, ("b2", cols, -way * s if s else 0, dx), at_x(dx))

    def relay_x(cols, s):
        for zz in ways_at(cols, s):
            for dx in (1, -1):
                arrived(block(zz, -dx, cols), ("b2", cols, zz, dx))
                if dx == cols[2]:
                    part = block(zz, -dx, cols)
                    send(part, part, ("b3", cols, zz), at_x(dx))

    def end_x(cols, s):
        for zz in ways_at(cols, s):
            arrived(block(zz, 2, cols), ("b3", cols, zz))

    def t_ready(cols):
        at = pl.ds(*cols)

        @pl.when(jnp.logical_not(source))
        def _():
            arrived(t_ref.at[own_t, at], ("ts", cols))

        for e in range(-REACH_T, REACH_T + 1):
            if e:
                send(t_ref.at[own_t, at], t_ref.at[pl.ds(8 * (REACH_T - e), 8), at], ("th", cols, e), along(e))

    def t_done(cols):
        at = pl.ds(*cols)
        for e in range(-REACH_T, REACH_T + 1):
            if e:
                arrived(t_ref.at[pl.ds(8 * (REACH_T - e), 8), at], ("th", cols, e))

    def tops(s):
        for k, cols in enumerate(T_CHUNKS[1:]):
            if s == TOPS_AT[k]:
                t_ready(cols)

    first, *rest = A_CHUNKS
    settle(SHIFTS[0])
    spread_x(first)
    settle(SHIFTS[1])
    for cols in B_CHUNKS:
        pass_block(cols, 0)
    settle(SHIFTS[2])
    for cols in rest:
        spread_x(cols)
    joined_x(first)
    pass_plane(first, 0)
    t_ready(T_CHUNKS[0])
    for cols in rest:
        joined_x(cols)
        pass_plane(cols, 0)
    for s in range(1, 5):
        pass_plane(first, s)
        for cols in B_CHUNKS:
            pass_block(cols, s)
        for cols in rest:
            pass_plane(cols, s)
        for cols in B_CHUNKS:
            relay_x(cols, s - 1)
        tops(s)
    t_done(T_CHUNKS[0])

    @pl.when(y == 0)
    def _():
        e_ref[core, ROWS : ROWS + 256] = r_ref[:, :NB]
        e_ref[core, ROWS + 256 :] = t_ref[:, :NB]
        for step in (1, 3, 2):
            copy(ext_rt, ext_rt, ("yr", step), (p, step * 2 + core), ("yr",)).start()

    @pl.when(y > 0)
    def _():
        arrived(ext_a, ("ya",))

    send(ext_a, ext_a, ("ca",), core_peer)
    for cols in B_CHUNKS:
        relay_x(cols, 4)
    tops(5)

    @pl.when(y > 0)
    def _():
        arrived(ext_rt, ("yr",))

    send(ext_rt, ext_rt, ("cr",), core_peer)
    tops(6)
    arrived(far_a, ("ca",))
    arrived(far_rt, ("cr",))
    weigh(e_ref, put_ref, slot_ref, low_ref, up_ref, w_ref, put16_ref, keep_ref, first_ref)
    for s in range(5):
        for cols in B_CHUNKS:
            end_x(cols, s)
    for cols in T_CHUNKS[1:]:
        t_done(cols)
    for c in pending:
        c.wait_send()

    @pl.when(y == 0)
    def _():
        for step in (1, 3, 2):
            copy(ext_a, ext_a, ("ya", step), (p, step * 2 + core), ("ya",)).wait_send()
            copy(ext_rt, ext_rt, ("yr", step), (p, step * 2 + core), ("yr",)).wait_send()

    @pl.when(source)
    def _():
        for cols in T_CHUNKS:
            at = pl.ds(*cols)
            for g in GROUP_ORDER:
                to = g // 2 * 4 + (p if g % 2 == 0 else 3 - p)
                copy(t_pack.at[pl.ds(8 * g, 8), at], t_ref.at[own_t, at], ("ts", cols, g), (to, q), ("ts", cols)).wait_send()


def gather(matrix, index, order, slot_hot, put, lower_inverse, upper_inverse):
    vmem = pl.BlockSpec(memory_space=pltpu.VMEM)
    return pl.pallas_call(
        gather_kernel,
        out_shape=[
            jax.ShapeDtypeStruct((256, COLS), F32),
            jax.ShapeDtypeStruct((TROWS, COLS), F32),
            *weights_of(TROWS),
        ],
        in_specs=[pl.BlockSpec(memory_space=pltpu.SMEM), vmem, vmem, vmem, vmem, vmem, pl.BlockSpec(memory_space=pl.ANY)],
        out_specs=[vmem] * 6,
        scratch_shapes=[
            pltpu.VMEM((ROWS, COLS), F32),
            pltpu.VMEM((8 * GROUPS_R, COLS), F32),
            pltpu.VMEM((8 * GROUPS_R, COLS), F32),
            pltpu.VMEM((NB, COLS), F32),
            pltpu.VMEM((2, EXT, NB), F32),
            pltpu.SemaphoreType.DMA((1,)),
            pltpu.SemaphoreType.DMA((COPIES,)),
            pltpu.SemaphoreType.DMA((COPIES,)),
        ],
        compiler_params=pltpu.CompilerParams(collective_id=0, has_side_effects=True, vmem_limit_bytes=48 << 20),
        name="gather_rows",
    )(index, order, slot_hot, put, lower_inverse, upper_inverse, matrix)


def split(x):
    high = x.astype(BF16)
    return high, (x - high.astype(F32)).astype(BF16)


def weigh(e_ref, put_ref, slot_ref, low_ref, up_ref, w_ref, put16_ref, keep_ref, first_ref):
    p, q = lax.axis_index("prow"), lax.axis_index("pcol")
    row, col = iota((NB, NB), 0), iota((NB, NB), 1)
    lower = [jnp.where(row > col, low_ref[t], jnp.where(row == col, 1.0, 0.0)) for t in range(2)]
    upper = [jnp.where(row <= col, up_ref[t], 0.0) for t in range(2)]
    put = put_ref[...]
    top = iota((ROWS, 1), 0) < NB
    at0, at1 = top & (p == 0), top & (p == 1)
    keep = jnp.where(at0 | at1, 0.0, 1.0 - jnp.sum(put, axis=1, keepdims=True))
    keep_ref[...] = jnp.broadcast_to(keep, (ROWS, NB))
    put16_ref[...] = put.astype(BF16)
    pi0, pi1 = slot_ref[:NB], slot_ref[NB:]
    g0, g1 = hp(lower[0], pi0), hp(lower[1], pi1)
    r0, r1 = e_ref[0, ROWS : ROWS + 256], e_ref[1, ROWS : ROWS + 256]
    k0 = hp(r0, upper[0])
    m1 = g1 - hp(hp(g1, k0), g0)
    u01 = hp(g0, r1)
    c0 = keep * e_ref[0, :ROWS] + hp(put, e_ref[0, ROWS + 256 :])
    c1 = keep * e_ref[1, :ROWS] + hp(put, e_ref[1, ROWS + 256 :])
    pis = jnp.where(p == 0, pi0, pi1)
    blank = jnp.zeros((ROWS - NB, NB), F32)
    c0 = jnp.where(at0 | at1, jnp.concatenate([hp(pis, r0), blank], 0), c0)
    c1 = jnp.where(at1, jnp.concatenate([hp(pi1, r1), blank], 0), c1)
    panel0 = hp(c0, upper[0])
    middle = c1 - hp(panel0, u01)
    panel1 = hp(middle, upper[1])
    w = hp(panel0, g0) + hp(panel1, m1)
    blank2 = jnp.zeros((ROWS - NB, 256), F32)
    w = jnp.where(at0 | at1, jnp.concatenate([-jnp.where(p == 0, g0, m1), blank2], 0), w)
    high, low = split(-w)
    w_ref[:, :256] = high
    w_ref[:, 256:512] = high
    w_ref[:, 512:] = low
    u01_tall = jnp.concatenate([u01, blank], 0)
    first0 = jnp.where(at0, c0, panel0)
    first1 = jnp.where(at0, u01_tall, jnp.where(at1, middle, panel1))
    first_ref[...] = jnp.where(q == 0, first0, first1)


def weights_of(trows):
    return [
        jax.ShapeDtypeStruct((ROWS, 768), BF16),
        jax.ShapeDtypeStruct((ROWS, trows), BF16),
        jax.ShapeDtypeStruct((ROWS, NB), F32),
        jax.ShapeDtypeStruct((ROWS, NB), F32),
    ]


WIDTH = 512


def finish_kernel(a_ref, r_ref, t_ref, w_ref, put16_ref, keep_ref, first_ref, o_ref):
    r_high, r_low = split(r_ref[...])
    t_high, t_low = split(t_ref[...])
    dot = functools.partial(jnp.dot, preferred_element_type=F32)
    rows = jnp.concatenate([r_high, r_low, r_high], 0)
    put16 = put16_ref[...]
    moved = dot(put16, t_high) + dot(put16, t_low)
    o_ref[...] = keep_ref[:, :1] * a_ref[...] + (moved + dot(w_ref[...], rows))

    @pl.when((pl.program_id(0) == 0) & (lax.axis_index("pcol") < 2))
    def _():
        o_ref[:, :NB] = first_ref[...]


def finish(matrix, rows, tops, weights):
    trows = tops.shape[0]
    whole = lambda *dims: pl.BlockSpec(dims, lambda i: (0,) * len(dims))
    wide = lambda n: pl.BlockSpec((n, WIDTH), lambda i: (0, i))
    return pl.pallas_call(
        finish_kernel,
        grid=(COLS // WIDTH,),
        out_shape=jax.ShapeDtypeStruct((ROWS, COLS), F32),
        in_specs=[wide(ROWS), wide(256), wide(trows), whole(ROWS, 768), whole(ROWS, trows), whole(ROWS, NB), whole(ROWS, NB)],
        out_specs=wide(ROWS),
        compiler_params=pltpu.CompilerParams(vmem_limit_bytes=48 << 20),
        name=f"finish_{trows}",
    )(matrix, rows, tops, *weights)


def any_pivots(matrix, meta, slot_hot, lower_inverse, upper_inverse):
    p, q = lax.axis_index("prow"), lax.axis_index("pcol")
    src, dest = meta[:2].reshape(256), meta[2:4].reshape(256)
    lines = jnp.arange(ROWS, dtype=I32)
    mine = hot((local_of(src)[:, None] == lines[None, :]) & (owner_of(src) == p)[:, None])
    rows = hp(hp(slot_hot.T, mine), matrix)
    section = (jnp.arange(256) // NB == p)[:, None]
    tops = jnp.where(section, jnp.concatenate([matrix[:NB], matrix[:NB]], 0), 0.0)
    rows, tops = lax.psum((rows, tops), "prow")
    here = (dest >= 0) & (owner_of(dest) == p)
    put = hot((local_of(dest)[None, :] == lines[:, None]) & here[None, :])
    held = jnp.concatenate([matrix[:, :NB], rows[:, :NB], tops[:, :NB]], 0)
    ext = jnp.stack([lax.psum(jnp.where(q == k, held, 0.0), "pcol") for k in range(2)])
    weights = pl.pallas_call(
        weigh,
        out_shape=weights_of(256),
        compiler_params=pltpu.CompilerParams(vmem_limit_bytes=48 << 20),
        name="weigh",
    )(ext, put, slot_hot, lower_inverse, upper_inverse)
    return finish(matrix, rows, tops, weights)


def spread_pivots(matrix, index, order, slot_hot, put, lower_inverse, upper_inverse):
    rows, tops, *weights = gather(matrix, index, order, slot_hot, put, lower_inverse, upper_inverse)
    return finish(matrix, rows, tops, weights)


def shards(matrix, pivots, lower_inverse, upper_inverse):
    fits, meta, index, order, slot_hot, put = plan(pivots)
    return lax.cond(
        fits[0] > 0,
        lambda: spread_pivots(matrix, index, order, slot_hot, put, lower_inverse, upper_inverse),
        lambda: any_pivots(matrix, meta, slot_hot, lower_inverse, upper_inverse),
    )


def solution(mesh):
    placed = (P("prow", "pcol"), P(), P(), P())
    return jax.shard_map(
        shards, mesh=mesh, in_specs=placed, out_specs=P("prow", "pcol"), check_vma=False
    )
```
